128 devices in a mesh: seq: 16 (over y_lo, z, core), head: 8 (over x, y_hi).
Axes of the slice: x: 4, y: 4 (y_hi: 2, y_lo: 2; y = y_hi * 2 + y_lo), z: 4, core: 2. Of those that a mesh axis runs over, the one named last changes fastest.
Arguments:
- hidden_states: bfloat16 [16384, 2048], P('seq'), may hold values from -6 to 6
- norm_gain: float32 [2048], replicated, may hold values from 0.1 to 1.9
- qkv_weight: bfloat16 [3, 2048, 2048], P(None, None, 'head'), may hold values from -1 to 1
- out_weight: bfloat16 [2048, 2048], P('head'), may hold values from -0.125 to 0.125
- selected_tiles: int32 [256, 32], P('seq'), may hold values from 0 to 255, as said below
- selected_count: int32 [256], P('seq'), may hold values from 1 to 32, as said below
Outputs:
- attended: bfloat16 [16384, 2048], P('seq', 'head')
The draws below stay inside these ranges and needn't reach their ends.
Inputs may be any that keep to these rules, and one draw needn't show every extreme that they name: `selected_tiles`: entries 0 to 4 of a query tile's list are the tile itself and the tiles one before, one after, two before and two after it, clamped to the first and last tile; later entries may name any tile and may repeat. Only the first selected_count entries of a list are used; in every draw some tiles use all 32 entries.
All inputs are finite; a program needn't handle non-finite values.
Results may differ from the reference program's by a relative error of at most 0.0055.
The reference program's roundings to bfloat16 on the way (of `normed`, `weights` and `context`) count: a program that leaves them out, or rounds other values in their place, can miss the bound.
Values may be sent and summed in bfloat16 or wider, within the bound.
No kernel may reach another device: no remote copies, remote signals or barrier semaphores. Data moves between devices by JAX's collectives and lax.ppermute only.
A program may use at most 128 MiB of HBM per device.

```python
import jax
import jax.numpy as jnp
from jax import lax

D = 2048
HEADS = 16
HD = 128
TILE = 64
SEL = 32
TOKENS = 16384


def draw_hidden_states(key, part):
    key = jax.random.fold_in(key, 21)
    states = jnp.clip(jax.random.normal(key, (TOKENS, D), jnp.float32), -6.0, 6.0)
    return states.astype(jnp.bfloat16)


def draw_qkv_weight(key, part):
    key = jax.random.fold_in(key, 22)
    scale = D ** (-0.5)
    matrices = jnp.clip(jax.random.normal(key, (3, D, D), jnp.float32), -6.0, 6.0) * scale
    return matrices.astype(jnp.bfloat16)


def draw_selected_tiles(key, part):
    key = jax.random.fold_in(key, 11)
    tile_total = TOKENS // TILE
    positions = jnp.arange(tile_total, dtype=jnp.int32)[:, None]
    reach_steps = jnp.array([0, -1, 1, -2, 2], dtype=jnp.int32)[None, :]
    nearby = jnp.clip(positions + reach_steps, 0, tile_total - 1)
    distant = jax.random.randint(key, (tile_total, SEL - 5), 0, tile_total, dtype=jnp.int32)
    return jnp.concatenate([nearby, distant], axis=1).astype(jnp.int32)


def draw_selected_count(key, part):
    key = jax.random.fold_in(key, 12)
    first_key, second_key, third_key = jax.random.split(key, 3)
    tile_total = TOKENS // TILE
    lower = jnp.minimum(jax.random.randint(first_key, (tile_total,), 1, SEL + 1, dtype=jnp.int32), jax.random.randint(second_key, (tile_total,), 1, SEL + 1, dtype=jnp.int32))
    anchor = jax.random.randint(third_key, (), 0, tile_total, dtype=jnp.int32)
    band_tiles = max(tile_total // 8, 1)
    busy_band = jnp.mod(jnp.arange(tile_total, dtype=jnp.int32) - anchor, tile_total) < band_tiles
    return jnp.where(busy_band, SEL, lower).astype(jnp.int32)


def shard_levels(key, extent, pieces, low, top_value):
    def one(dim, parts):
        steps = jax.random.uniform(jax.random.fold_in(jax.random.fold_in(key, 6), dim), (parts,), jnp.float32, low / len(pieces), top_value / len(pieces))
        return jnp.repeat(jnp.exp(steps), extent[dim] // parts).reshape((-1,) + (1,) * (len(extent) - dim - 1))

    level = one(*pieces[0])
    for cut in pieces[1:]:
        level = level * one(*cut)
    return level


def normal_values(stream_key, dims, scale, limit, shards=(), held_as=jnp.bfloat16):
    values = jax.random.normal(stream_key, dims, jnp.float32) * scale
    if len(shards) > 0:
        values = shard_levels(stream_key, dims, shards, -0.22, 0.18) * values
    return jnp.clip(values, min=-limit, max=limit).astype(held_as)


def setup_inputs(seed: int = 0) -> dict:
    streams_of = jax.random.split(jax.random.key(seed), 7)
    return {
        "hidden_states": draw_hidden_states(jax.random.fold_in(streams_of[6], 71), 0),
        "norm_gain": jnp.clip(1.0 + 0.18 * jax.random.normal(streams_of[1], (D,), jnp.float32), 0.1, 1.9),
        "qkv_weight": draw_qkv_weight(jax.random.fold_in(streams_of[6], 71), 0),
        "out_weight": normal_values(streams_of[3], (D, D), D ** -0.5, 0.125, ((0, 8),)),
        "selected_tiles": draw_selected_tiles(jax.random.fold_in(streams_of[6], 71), 0),
        "selected_count": draw_selected_count(jax.random.fold_in(streams_of[6], 71), 0),
    }


EPSILON = 1e-06
NEGATIVE = -1e+30

def normalize(hidden_states, norm_gain):
    values = hidden_states.astype(jnp.float32)
    spread = lax.optimization_barrier(jnp.mean(values * values, axis=-1, keepdims=True))
    return (values * lax.rsqrt(spread + EPSILON) * norm_gain).astype(jnp.bfloat16)

def reference(hidden_states, norm_gain, qkv_weight, out_weight, selected_tiles, selected_count):
    normed = normalize(hidden_states, norm_gain)
    projected = [jnp.dot(normed, qkv_weight[member], preferred_element_type=jnp.float32).astype(jnp.bfloat16) for member in range(3)]
    tile_total = TOKENS // TILE
    query_tiles = projected[0].reshape(tile_total, TILE, HEADS, HD)
    key_tiles = projected[1].reshape(tile_total, TILE, HEADS, HD)
    value_tiles = projected[2].reshape(tile_total, TILE, HEADS, HD)
    scaling = HD ** (-0.5)

    def attend(operands):
        queries, chosen, tile_count = operands
        keyset = key_tiles[chosen].reshape(SEL * TILE, HEADS, HD).astype(jnp.float32)
        valueset = value_tiles[chosen].reshape(SEL * TILE, HEADS, HD).astype(jnp.float32)
        scores = jnp.einsum('qhd,khd->hqk', queries.astype(jnp.float32), keyset) * scaling
        usable = jnp.repeat(jnp.arange(SEL) < tile_count, TILE)[None, None, :]
        scores = jnp.where(usable, scores, NEGATIVE)
        highest = lax.optimization_barrier(jnp.max(scores, axis=-1, keepdims=True))
        weights = jnp.where(usable, jnp.exp(scores - highest), 0.0)
        totals = lax.optimization_barrier(jnp.sum(weights, axis=-1))
        rounded = lax.optimization_barrier(weights.astype(jnp.bfloat16)).astype(jnp.float32)
        summed = jnp.einsum('hqk,khd->qhd', rounded, valueset)
        return (summed / jnp.transpose(totals)[:, :, None]).astype(jnp.bfloat16)
    context = lax.map(attend, (query_tiles, selected_tiles, selected_count)).reshape(TOKENS, D)
    return jnp.dot(context, out_weight, preferred_element_type=jnp.float32).astype(jnp.bfloat16)
```

```python
import functools

import jax
import jax.numpy as jnp
from jax import lax
from jax.experimental import pallas as pl
from jax.experimental.pallas import tpu as pltpu
from jax.sharding import PartitionSpec as P

HD = 128
TILE = 64
SEL = 32
EPSILON = 1e-06
NEGATIVE = -1e30
EXPONENT = float(HD**-0.5 * 1.4426950408889634)
AXES = ("seq", "head")
GROUP = 4
ROWS = 4
VM = pl.BlockSpec(memory_space=pltpu.VMEM)
SM = pl.BlockSpec(memory_space=pltpu.SMEM)
ANY = pl.BlockSpec(memory_space=pl.ANY)


def coords(i):
    s, h = divmod(i, 8)
    yl, r = divmod(s, 8)
    z, c = divmod(r, 2)
    x, yh = divmod(h, 2)
    return x, yh, yl, z, c


def index(x, yh, yl, z, c):
    return ((yl * 4 + z) * 2 + c) * 8 + x * 2 + yh


def move(array, dx=0, dyh=0, dyl=0, dz=0, dc=0):
    pairs = []
    for i in range(128):
        x, yh, yl, z, c = coords(i)
        pairs.append((i, index((x + dx) % 4, yh ^ dyh, yl ^ dyl, (z + dz) % 4, c ^ dc)))
    return lax.ppermute(array, AXES, pairs)


def project_kernel(half_ref, h_ref, gain_ref, ko, vo, km, vm, qm, qo, kvo_ref, kvm_ref, qm_ref, qo_ref):
    values = h_ref[...].astype(jnp.float32)
    spread = jnp.mean(values * values, axis=-1, keepdims=True)
    normed = (values * lax.rsqrt(spread + EPSILON) * gain_ref[...]).astype(jnp.bfloat16)

    def pair(a, b):
        weight = jnp.concatenate([a[0], b[0]], axis=1)
        return jnp.dot(normed, weight, preferred_element_type=jnp.float32).astype(jnp.bfloat16)

    kvo_ref[...] = pair(ko, vo)
    kvm_ref[...] = pair(km, vm)
    both = pair(qm, qo)
    qm_ref[...] = both[:, :HD]
    qo_ref[...] = both[:, HD:]


def project(hidden, gain, weight, yl):
    rows, width = hidden.shape
    block = 256

    def part(member, flip):
        return pl.BlockSpec(
            (1, width, HD), lambda i, half: (member, 0, half[0] ^ flip)
        )

    out = lambda n: pl.BlockSpec((block, n), lambda i, half: (i, 0))
    return pl.pallas_call(
        project_kernel,
        grid_spec=pltpu.PrefetchScalarGridSpec(
            num_scalar_prefetch=1,
            grid=(rows // block,),
            in_specs=[
                pl.BlockSpec((block, width), lambda i, half: (i, 0)),
                pl.BlockSpec((1, width), lambda i, half: (0, 0)),
                part(1, 1), part(2, 1), part(1, 0), part(2, 0), part(0, 0), part(0, 1),
            ],
            out_specs=[out(256), out(256), out(HD), out(HD)],
        ),
        out_shape=[
            jax.ShapeDtypeStruct((rows, 256), jnp.bfloat16),
            jax.ShapeDtypeStruct((rows, 256), jnp.bfloat16),
            jax.ShapeDtypeStruct((rows, HD), jnp.bfloat16),
            jax.ShapeDtypeStruct((rows, HD), jnp.bfloat16),
        ],
        compiler_params=pltpu.CompilerParams(vmem_limit_bytes=40 * 2**20),
        cost_estimate=pl.CostEstimate(
            flops=2 * rows * width * 768, bytes_accessed=9 * 2**20, transcendentals=0
        ),
        name="project",
    )(jnp.reshape(yl, (1,)).astype(jnp.int32), hidden, gain.reshape(1, width),
      weight, weight, weight, weight, weight, weight)


def gathered(kv, list_ref, tile, group, half):
    parts = []
    for j in range(GROUP):
        row = pl.multiple_of(list_ref[tile, group * GROUP + j] * TILE, TILE)
        parts.append(kv[pl.ds(row, TILE), half * HD : half * HD + HD])
    return jnp.concatenate(parts, axis=0)


def query_rows(tile):
    return pl.ds(pl.multiple_of(tile * TILE, TILE), TILE)


def score_tile(tile, groups, list_ref, count_ref, q_ref, kv):
    q = q_ref[query_rows(tile), :]
    lane = lax.broadcasted_iota(jnp.int32, (TILE, GROUP * TILE), 1)
    out = []
    for g in range(groups):
        s = lax.dot_general(
            q, gathered(kv, list_ref, tile, g, 0), (((1,), (1,)), ((), ())),
            preferred_element_type=jnp.float32,
        )
        out.append(jnp.where(lane < (count_ref[tile] - GROUP * g) * TILE, s, NEGATIVE))
    return out


def highest_of(scores):
    parts = [s[:, k : k + HD] for s in scores for k in range(0, GROUP * TILE, HD)]
    return jnp.max(functools.reduce(jnp.maximum, parts), axis=-1, keepdims=True)


def context_tile(tile, scores, highest, list_ref, kv, o_ref):
    totals = summed = 0.0
    for g, s in enumerate(scores):
        weights = jnp.exp2((s - highest) * EXPONENT)
        for k in range(0, GROUP * TILE, HD):
            totals = totals + weights[:, k : k + HD]
        summed = summed + jnp.dot(
            weights.astype(jnp.bfloat16), gathered(kv, list_ref, tile, g, 1),
            preferred_element_type=jnp.float32,
        )
    totals = jnp.sum(totals, axis=-1, keepdims=True)
    o_ref[query_rows(tile), :] = (summed / totals).astype(jnp.bfloat16)


def attend_kernel(list_ref, count_ref, order_ref, qm_ref, qp_ref, *rest):
    pieces, (o_ref, kv, q_ref, sems) = rest[:16], rest[16:]
    rows = pieces[0].shape[0]
    copies = [
        pltpu.make_async_copy(piece, kv.at[pl.ds(k * rows, rows)], sems.at[k])
        for k, piece in enumerate(pieces)
    ]
    for copy in copies:
        copy.start()
    q_ref[:rows, :] = qm_ref[...]
    q_ref[rows:, :] = qp_ref[...]
    for copy in copies:
        copy.wait()
    tiles = q_ref.shape[0] // TILE

    @pl.loop(0, tiles // ROWS)
    def _(block):
        ids = [order_ref[block * ROWS + j] for j in range(ROWS)]
        longest = functools.reduce(jnp.maximum, [count_ref[t] for t in ids])
        needed = (longest + GROUP - 1) // GROUP
        for groups in range(1, SEL // GROUP + 1):

            @pl.when(needed == groups)
            def _():
                scores = [score_tile(t, groups, list_ref, count_ref, q_ref, kv) for t in ids]
                tops = [highest_of(s) for s in scores]
                for t, s, top in zip(ids, scores, tops):
                    context_tile(t, s, top, list_ref, kv, o_ref)


def attend(lists, counts, order, qm, qp, pieces):
    rows = qm.shape[0]
    return pl.pallas_call(
        attend_kernel,
        out_shape=jax.ShapeDtypeStruct((2 * rows, HD), jnp.bfloat16),
        in_specs=[SM, SM, SM, VM, VM] + [ANY] * 16,
        out_specs=VM,
        scratch_shapes=[
            pltpu.VMEM((16 * rows, 2 * HD), jnp.bfloat16),
            pltpu.VMEM((2 * rows, HD), jnp.bfloat16),
            pltpu.SemaphoreType.DMA((16,)),
        ],
        compiler_params=pltpu.CompilerParams(vmem_limit_bytes=48 * 2**20),
        cost_estimate=pl.CostEstimate(
            flops=4 * 2 * rows * SEL * TILE * HD, bytes_accessed=10 * 2**20,
            transcendentals=2 * rows * SEL * TILE,
        ),
        name="attend",
    )(lists, counts, order, qm, qp, *pieces)


def out_kernel(*refs):
    mine, partner, weights = refs[0:4], refs[4:8], refs[8:12]
    own_ref, swap_yh_ref, swap_yl_ref, swap_both_ref = refs[12:]
    weight = jnp.concatenate([w[...] for w in weights], axis=0)
    half = weight.shape[1] // 2
    m = jnp.dot(
        jnp.concatenate([r[...] for r in mine], axis=1), weight,
        preferred_element_type=jnp.float32,
    )
    own_ref[...] = m[:, :half]
    swap_yh_ref[...] = m[:, half:].astype(jnp.bfloat16)
    p = jnp.dot(
        jnp.concatenate([r[...] for r in partner], axis=1), weight,
        preferred_element_type=jnp.float32,
    )
    swap_yl_ref[...] = p[:, :half].astype(jnp.bfloat16)
    swap_both_ref[...] = p[:, half:].astype(jnp.bfloat16)


def out_project(contexts, weights):
    rows = contexts[0].shape[0] // 2
    block = 256
    steps = rows // block
    lower = pl.BlockSpec((block, HD), lambda i: (i, 0))
    upper = pl.BlockSpec((block, HD), lambda i: (i + steps, 0))
    whole = pl.BlockSpec(weights[0].shape, lambda i: (0, 0))
    out = pl.BlockSpec((block, 256), lambda i: (i, 0))
    return pl.pallas_call(
        out_kernel,
        grid=(steps,),
        in_specs=[lower] * 4 + [upper] * 4 + [whole] * 4,
        out_specs=[out] * 4,
        out_shape=[jax.ShapeDtypeStruct((rows, 256), jnp.float32)]
        + [jax.ShapeDtypeStruct((rows, 256), jnp.bfloat16)] * 3,
        cost_estimate=pl.CostEstimate(
            flops=2 * 2 * rows * 512 * 512, bytes_accessed=6 * 2**20, transcendentals=0
        ),
        name="out_project",
    )(*contexts, *contexts, *weights)


def per_device(hidden_states, norm_gain, qkv_weight, out_weight, selected_tiles, selected_count):
    seq = lax.axis_index("seq")
    head = lax.axis_index("head")
    yl, z, core = seq // 8, (seq % 8) // 2, seq % 2
    yh = head % 2

    def weight_block(x):
        own = lax.dynamic_slice(out_weight, (yl * HD, (x * 2 + yh) * 256), (HD, 256))
        other = lax.dynamic_slice(out_weight, (yl * HD, (x * 2 + 1 - yh) * 256), (HD, 256))
        return jnp.concatenate([own, other], axis=1)

    x = head // 2
    steps = (0, 1, 3, 2)
    out_weights = [
        weight_block(x) if d == 0 else move(weight_block((x + d) % 4), dx=d) for d in steps
    ]

    rows_here = selected_tiles.shape[0]
    packed = jnp.concatenate(
        [selected_tiles, selected_count[:, None], jnp.zeros((rows_here, 95), jnp.int32)], axis=1
    )
    packed = jnp.concatenate([packed, move(packed, dyl=1)], axis=0)
    counts = packed[:, SEL]
    tile = packed[:, :SEL]
    slab = tile // rows_here
    place = (((slab % 8 // 2 - z) % 4) * 2 + ((slab // 8) ^ yl)) * 2 + ((slab % 2) ^ core)
    lists = place * rows_here + tile % rows_here
    n = counts.shape[0]
    ids = jnp.arange(n, dtype=jnp.int32)
    before = (counts[None, :] > counts[:, None]) | (
        (counts[None, :] == counts[:, None]) & (ids[None, :] < ids[:, None])
    )
    rank = jnp.sum(before.astype(jnp.int32), axis=1)
    order = jnp.sum(jnp.where(rank[None, :] == ids[:, None], ids[None, :], 0), axis=1)

    kvo, kvm, qm, qo = project(hidden_states, norm_gain, qkv_weight, yl)

    kvp = move(kvo, dyl=1)
    up_m = move(kvm, dz=1)
    down_m = move(kvm, dz=-1)
    up_p = move(kvp, dz=1)
    down_p = move(kvp, dz=-1)
    far_m = move(up_m, dz=1)
    far_p = move(down_p, dz=-1)
    qp = move(qo, dyl=1)
    pieces = []
    for m, p in ((kvm, kvp), (down_m, down_p), (far_m, far_p), (up_m, up_p)):
        pieces += [m, move(m, dc=1), p, move(p, dc=1)]

    context = attend(lists, counts, order, qm, qp, pieces)

    contexts = [context] + [move(context, dx=d) for d in (1, 3, 2)]
    own, to_yh, to_yl, to_both = out_project(contexts, out_weights)
    total = own
    for block in (move(to_yl, dyl=1), move(to_both, dyl=1, dyh=1), move(to_yh, dyh=1)):
        total = total + block.astype(jnp.float32)
    return total.astype(jnp.bfloat16)


def solution(mesh):
    return jax.shard_map(
        per_device,
        mesh=mesh,
        in_specs=(
            P("seq", None),
            P(),
            P(None, None, "head"),
            P("head", None),
            P("seq", None),
            P("seq"),
        ),
        out_specs=P("seq", "head"),
        check_vma=False,
    )
```

```python
import functools

import jax
import jax.numpy as jnp
from jax import lax
from jax.experimental import pallas as pl
from jax.experimental.pallas import tpu as pltpu
from jax.sharding import PartitionSpec as P

D = 2048
HD = 128
TILE = 64
SEL = 32
EPSILON = 1e-06
NEGATIVE = -1e30
EXPONENT = float(HD**-0.5 * 1.4426950408889634)
AXES = ("seq", "head")
GROUP = 4
ROWS = 4
VM = pl.BlockSpec(memory_space=pltpu.VMEM)
SM = pl.BlockSpec(memory_space=pltpu.SMEM)
ANY = pl.BlockSpec(memory_space=pl.ANY)
PROJECT_VMEM = 60 * 2**20
ATTEND_VMEM = 24 * 2**20
OUT_VMEM = 12 * 2**20
CHUNKS = 2


def coords(i):
    s, h = divmod(i, 8)
    yl, r = divmod(s, 8)
    z, c = divmod(r, 2)
    x, yh = divmod(h, 2)
    return x, yh, yl, z, c


def index(x, yh, yl, z, c):
    return ((yl * 4 + z) * 2 + c) * 8 + x * 2 + yh


def move(array, dx=0, dyh=0, dyl=0, dz=0, dc=0):
    pairs = []
    for i in range(128):
        x, yh, yl, z, c = coords(i)
        pairs.append((i, index((x + dx) % 4, yh ^ dyh, yl ^ dyl, (z + dz) % 4, c ^ dc)))
    return lax.ppermute(array, AXES, pairs)


def first_kernel(half_ref, h_ref, gain_ref, ko, vo, km, vm, normed_ref, kvo_ref, kvm_ref):
    values = h_ref[...].astype(jnp.float32)
    spread = jnp.mean(values * values, axis=-1, keepdims=True)
    normed = (values * lax.rsqrt(spread + EPSILON) * gain_ref[...]).astype(jnp.bfloat16)
    normed_ref[...] = normed
    for k_ref, v_ref, out_ref in ((ko, vo, kvo_ref), (km, vm, kvm_ref)):
        weight = jnp.concatenate([k_ref[0], v_ref[0]], axis=1)
        both = jnp.dot(normed, weight, preferred_element_type=jnp.float32)
        out_ref[...] = both.astype(jnp.bfloat16)


def second_kernel(half_ref, normed_ref, qm, qo, qm_ref, qo_ref):
    weight = jnp.concatenate([qm[0], qo[0]], axis=1)
    both = jnp.dot(normed_ref[...], weight, preferred_element_type=jnp.float32)
    both = both.astype(jnp.bfloat16)
    qm_ref[...] = both[:, :HD]
    qo_ref[...] = both[:, HD:]


def project(kernel, operands, weight, half, parts, outs):
    rows, width = operands[0].shape
    block = 512

    def part(member, flip):
        return pl.BlockSpec((1, width, HD), lambda i, half: (member, 0, half[0] ^ flip))

    def rows_of(n):
        return pl.BlockSpec((block, n), lambda i, half: (i, 0))

    return pl.pallas_call(
        kernel,
        grid_spec=pltpu.PrefetchScalarGridSpec(
            num_scalar_prefetch=1,
            grid=(rows // block,),
            in_specs=[rows_of(width)]
            + [pl.BlockSpec((1, width), lambda i, half: (0, 0))] * (len(operands) - 1)
            + [part(*p) for p in parts],
            out_specs=[rows_of(n) for n in outs],
        ),
        out_shape=[jax.ShapeDtypeStruct((rows, n), jnp.bfloat16) for n in outs],
        compiler_params=pltpu.CompilerParams(vmem_limit_bytes=PROJECT_VMEM),
        cost_estimate=pl.CostEstimate(
            flops=2 * rows * width * HD * len(parts), bytes_accessed=9 * 2**20, transcendentals=0
        ),
        name="project",
    )(half, *operands, *[weight] * len(parts))


def gathered(kv_ref, list_ref, tile, group, half):
    parts = []
    for j in range(GROUP):
        row = pl.multiple_of(list_ref[tile, group * GROUP + j] * TILE, TILE)
        parts.append(kv_ref[pl.ds(row, TILE), half * HD : half * HD + HD])
    return jnp.concatenate(parts, axis=0)


def query_rows(tile):
    return pl.ds(pl.multiple_of(tile * TILE, TILE), TILE)


def score_tile(tile, groups, list_ref, count_ref, q_ref, kv_ref):
    q = q_ref[query_rows(tile), :]
    lane = lax.broadcasted_iota(jnp.int32, (TILE, GROUP * TILE), 1)
    out = []
    for g in range(groups):
        s = lax.dot_general(
            q, gathered(kv_ref, list_ref, tile, g, 0), (((1,), (1,)), ((), ())),
            preferred_element_type=jnp.float32,
        )
        out.append(jnp.where(lane < (count_ref[tile] - GROUP * g) * TILE, s, NEGATIVE))
    return out


def highest_of(scores):
    parts = [s[:, k : k + HD] for s in scores for k in range(0, GROUP * TILE, HD)]
    return jnp.max(functools.reduce(jnp.maximum, parts), axis=-1, keepdims=True)


def context_tile(tile, scores, highest, list_ref, kv_ref, o_ref):
    totals = summed = 0.0
    for g, s in enumerate(scores):
        weights = jnp.exp2((s - highest) * EXPONENT)
        for k in range(0, GROUP * TILE, HD):
            totals = totals + weights[:, k : k + HD]
        summed = summed + jnp.dot(
            weights.astype(jnp.bfloat16), gathered(kv_ref, list_ref, tile, g, 1),
            preferred_element_type=jnp.float32,
        )
    totals = jnp.sum(totals, axis=-1, keepdims=True)
    o_ref[query_rows(tile), :] = (summed / totals).astype(jnp.bfloat16)


def attend_kernel(list_ref, count_ref, order_ref, qm_ref, qp_ref, *rest):
    pieces, rest = rest[:16], rest[16:]
    outs, (kv_ref, q_ref, o_ref, sems) = rest[: 2 * CHUNKS], rest[2 * CHUNKS :]
    rows = pieces[0].shape[0]
    copies = [
        pltpu.make_async_copy(piece, kv_ref.at[pl.ds(k * rows, rows)], sems.at[k])
        for k, piece in enumerate(pieces)
    ]
    for copy in copies:
        copy.start()
    q_ref[:rows, :] = qm_ref[...]
    q_ref[rows:, :] = qp_ref[...]
    for copy in copies:
        copy.wait()
    tiles = q_ref.shape[0] // TILE

    @pl.loop(0, tiles // ROWS)
    def _(block):
        ids = [order_ref[block * ROWS + j] for j in range(ROWS)]
        longest = functools.reduce(jnp.maximum, [count_ref[t] for t in ids])
        needed = (longest + GROUP - 1) // GROUP
        for groups in range(1, SEL // GROUP + 1):

            @pl.when(needed == groups)
            def _():
                scores = [score_tile(t, groups, list_ref, count_ref, q_ref, kv_ref) for t in ids]
                tops = [highest_of(s) for s in scores]
                for t, s, top in zip(ids, scores, tops):
                    context_tile(t, s, top, list_ref, kv_ref, o_ref)


    part = outs[0].shape[0]
    for k, out in enumerate(outs):
        out[...] = o_ref[k * part : (k + 1) * part, :]


def attend(lists, counts, order, qm, qp, pieces):
    rows = qm.shape[0]
    part = jax.ShapeDtypeStruct((rows // CHUNKS, HD), jnp.bfloat16)
    return pl.pallas_call(
        attend_kernel,
        out_shape=[part] * (2 * CHUNKS),
        in_specs=[SM, SM, SM, VM, VM] + [ANY] * 16,
        out_specs=[VM] * (2 * CHUNKS),
        scratch_shapes=[
            pltpu.VMEM((16 * rows, 2 * HD), jnp.bfloat16),
            pltpu.VMEM((2 * rows, HD), jnp.bfloat16),
            pltpu.VMEM((2 * rows, HD), jnp.bfloat16),
            pltpu.SemaphoreType.DMA((16,)),
        ],
        compiler_params=pltpu.CompilerParams(vmem_limit_bytes=ATTEND_VMEM),
        cost_estimate=pl.CostEstimate(
            flops=4 * 2 * rows * SEL * TILE * HD, bytes_accessed=10 * 2**20,
            transcendentals=2 * rows * SEL * TILE,
        ),
        name="attend",
    )(lists, counts, order, qm, qp, *pieces)


def out_kernel(c0, c1, c2, c3, upper_ref, lower_ref, own_ref, *outs):
    context = jnp.concatenate([c0[...], c1[...], c2[...], c3[...]], axis=1)
    weight = jnp.concatenate([upper_ref[...], lower_ref[...]], axis=0)
    own_ref[...] = jnp.dot(context, weight[:, :256], preferred_element_type=jnp.float32)
    for k, out in enumerate(outs):
        part = weight[:, 256 * (k + 1) : 256 * (k + 2)]
        out[...] = jnp.dot(context, part, preferred_element_type=jnp.float32).astype(out.dtype)


def out_project(contexts, weights):
    rows = contexts[0].shape[0]
    return pl.pallas_call(
        out_kernel,
        in_specs=[VM] * 6,
        out_specs=[VM] * 4,
        out_shape=[jax.ShapeDtypeStruct((rows, 256), jnp.float32)]
        + [jax.ShapeDtypeStruct((rows, 256), jnp.bfloat16)] * 3,
        compiler_params=pltpu.CompilerParams(vmem_limit_bytes=OUT_VMEM),
        cost_estimate=pl.CostEstimate(
            flops=2 * rows * 512 * 1024, bytes_accessed=3 * 2**20, transcendentals=0
        ),
        name="out_project",
    )(*contexts, *weights)


def sum_kernel(*refs):
    own_ref, blocks, out_ref = refs[0], refs[1:4], refs[-1]
    total = own_ref[...]
    for block in blocks:
        total = total + block[...].astype(jnp.float32)
    out_ref[...] = total.astype(out_ref.dtype)


def sum_part(own, blocks, part, before):
    rows, columns = own.shape
    whole = pl.BlockSpec((rows, columns), lambda i: (0, 0))
    return pl.pallas_call(
        sum_kernel,
        grid=(1,),
        in_specs=[whole] * 4 + [ANY] * len(before),
        out_specs=pl.BlockSpec((rows, columns), lambda i: (part, 0)),
        out_shape=jax.ShapeDtypeStruct((rows * CHUNKS, columns), jnp.bfloat16),
        input_output_aliases={4: 0} if before else {},
        compiler_params=pltpu.CompilerParams(vmem_limit_bytes=OUT_VMEM),
        name="sum_part",
    )(own, *blocks, *before)


def per_device(hidden_states, norm_gain, qkv_weight, out_weight, selected_tiles, selected_count):
    seq = lax.axis_index("seq")
    head = lax.axis_index("head")
    yl, z, core = seq // 8, (seq % 8) // 2, seq % 2
    yh = head % 2

    x = head // 2

    def weight_rows(flip):
        columns = []
        for d in (0, 1, 3, 2):
            start = ((x + d) % 4 * 2 + (yh ^ flip)) * 256
            columns.append(lax.dynamic_slice(out_weight, (0, start), (256, 256)))
        both = jnp.concatenate(columns, axis=1)
        return jnp.where(yl == 0, both, jnp.roll(both, HD, axis=0))

    own_weight = weight_rows(0)
    sent_weight = weight_rows(1)

    rows_here = selected_tiles.shape[0]
    packed = jnp.concatenate(
        [selected_tiles, selected_count[:, None], jnp.zeros((rows_here, 95), jnp.int32)], axis=1
    )
    packed = jnp.concatenate([packed, move(packed, dyl=1)], axis=0)
    counts = packed[:, SEL]
    tile = packed[:, :SEL]
    slab = tile // rows_here
    place = (((slab % 8 // 2 - z) % 4) * 2 + ((slab // 8) ^ yl)) * 2 + ((slab % 2) ^ core)
    lists = place * rows_here + tile % rows_here
    n = counts.shape[0]
    ids = jnp.arange(n, dtype=jnp.int32)
    before = (counts[None, :] > counts[:, None]) | (
        (counts[None, :] == counts[:, None]) & (ids[None, :] < ids[:, None])
    )
    rank = jnp.sum(before.astype(jnp.int32), axis=1)
    order = jnp.sum(jnp.where(rank[None, :] == ids[:, None], ids[None, :], 0), axis=1)

    barrier = lax.optimization_barrier
    half = jnp.reshape(yl, (1,)).astype(jnp.int32)
    gain = norm_gain.reshape(1, -1)
    normed, kvo, kvm = project(
        first_kernel, (hidden_states, gain), qkv_weight, half,
        ((1, 1), (2, 1), (1, 0), (2, 0)), (D, 2 * HD, 2 * HD),
    )
    qm, qo = project(second_kernel, (normed,), qkv_weight, half, ((0, 0), (0, 1)), (HD, HD))

    kvp = move(kvo, dyl=1)
    up_m, down_m, core_m = move(kvm, dz=1), move(kvm, dz=-1), move(kvm, dc=1)
    kvp, sent_weight, lists, counts, order = barrier((kvp, sent_weight, lists, counts, order))
    up_p, down_p = move(kvp, dz=1), move(kvp, dz=-1)
    core_up_m, core_down_m = move(up_m, dc=1), move(down_m, dc=1)
    other_weight = move(sent_weight, dyh=1)
    up_m, down_m, up_p, down_p, kvp, qo, core_m, core_up_m, core_down_m, other_weight = barrier(
        (up_m, down_m, up_p, down_p, kvp, qo, core_m, core_up_m, core_down_m, other_weight)
    )
    far_m, far_p = move(up_m, dz=1), move(down_p, dz=-1)
    qp = move(qo, dyl=1)
    core_up_p, core_down_p, core_p = move(up_p, dc=1), move(down_p, dc=1), move(kvp, dc=1)
    far_m, far_p, qp, core_up_p, core_down_p, core_p = barrier(
        (far_m, far_p, qp, core_up_p, core_down_p, core_p)
    )
    core_far_m, core_far_p = move(far_m, dc=1), move(far_p, dc=1)
    parts = attend(
        lists, counts, order, qm, qp,
        (kvm, core_m, kvp, core_p, down_m, core_down_m, down_p, core_down_p,
         far_m, core_far_m, far_p, core_far_p, up_m, core_up_m, up_p, core_up_p),
    )

    weights = (own_weight, other_weight)
    before = ()
    for k, (mine, partner) in enumerate(zip(parts[:CHUNKS], parts[CHUNKS:])):
        contexts = (
            mine, move(partner, dyl=1), move(mine, dyh=1), move(partner, dyl=1, dyh=1)
        )
        own, *sent = out_project(contexts, weights)
        blocks = [move(block, dx=d) for d, block in zip((1, 3, 2), sent)]
        before = (sum_part(own, blocks, k, before),)
    return before[0]


def solution(mesh):
    return jax.shard_map(
        per_device,
        mesh=mesh,
        in_specs=(
            P("seq", None),
            P(),
            P(None, None, "head"),
            P("head", None),
            P("seq", None),
            P("seq"),
        ),
        out_specs=P("seq", "head"),
        check_vma=False,
    )
```

```python
import functools

import jax
import jax.numpy as jnp
from jax import lax
from jax.experimental import pallas as pl
from jax.experimental.pallas import tpu as pltpu
from jax.sharding import PartitionSpec as P

D = 2048
HD = 128
TILE = 64
SEL = 32
EPSILON = 1e-06
NEGATIVE = -1e30
EXPONENT = float(HD**-0.5 * 1.4426950408889634)
AXES = ("seq", "head")
GROUP = 4
ROWS = 4
VM = pl.BlockSpec(memory_space=pltpu.VMEM)
SM = pl.BlockSpec(memory_space=pltpu.SMEM)
ANY = pl.BlockSpec(memory_space=pl.ANY)
HBM = pl.BlockSpec(memory_space=pltpu.HBM)
ATTEND_VMEM = 24 * 2**20
OUT_VMEM = 12 * 2**20
CHUNKS = 2


def coords(i):
    s, h = divmod(i, 8)
    yl, r = divmod(s, 8)
    z, c = divmod(r, 2)
    x, yh = divmod(h, 2)
    return x, yh, yl, z, c


def index(x, yh, yl, z, c):
    return ((yl * 4 + z) * 2 + c) * 8 + x * 2 + yh


def move(array, dx=0, dyh=0, dyl=0, dz=0, dc=0):
    pairs = []
    for i in range(128):
        x, yh, yl, z, c = coords(i)
        pairs.append((i, index((x + dx) % 4, yh ^ dyh, yl ^ dyl, (z + dz) % 4, c ^ dc)))
    return lax.ppermute(array, AXES, pairs)


def normalize(h_ref, gain_ref):
    values = h_ref[...].astype(jnp.float32)
    spread = jnp.mean(values * values, axis=-1, keepdims=True)
    return (values * lax.rsqrt(spread + EPSILON) * gain_ref[...]).astype(jnp.bfloat16)


def keys_kernel(half_ref, h_ref, gain_ref, ko, vo, km, vm, kvo_ref, kvm_ref):
    normed = normalize(h_ref, gain_ref)
    for k_ref, v_ref, out_ref in ((ko, vo, kvo_ref), (km, vm, kvm_ref)):
        weight = jnp.concatenate([k_ref[0], v_ref[0]], axis=1)
        both = jnp.dot(normed, weight, preferred_element_type=jnp.float32)
        out_ref[...] = both.astype(jnp.bfloat16)


def queries_kernel(half_ref, h_ref, gain_ref, qm, qo, qm_ref, qo_ref):
    weight = jnp.concatenate([qm[0], qo[0]], axis=1)
    both = jnp.dot(normalize(h_ref, gain_ref), weight, preferred_element_type=jnp.float32)
    both = both.astype(jnp.bfloat16)
    qm_ref[...] = both[:, :HD]
    qo_ref[...] = both[:, HD:]


def project(kernel, operands, weight, half, parts, outs, vmem):
    rows, width = operands[0].shape
    block = 512

    def part(member, flip):
        return pl.BlockSpec((1, width, HD), lambda i, half: (member, 0, half[0] ^ flip))

    def rows_of(n):
        return pl.BlockSpec((block, n), lambda i, half: (i, 0))

    return pl.pallas_call(
        kernel,
        grid_spec=pltpu.PrefetchScalarGridSpec(
            num_scalar_prefetch=1,
            grid=(rows // block,),
            in_specs=[rows_of(width)]
            + [pl.BlockSpec((1, width), lambda i, half: (0, 0))] * (len(operands) - 1)
            + [part(*p) for p in parts],
            out_specs=[rows_of(n) for n in outs],
        ),
        out_shape=[jax.ShapeDtypeStruct((rows, n), jnp.bfloat16) for n in outs],
        compiler_params=pltpu.CompilerParams(vmem_limit_bytes=vmem),
        cost_estimate=pl.CostEstimate(flops=1024, bytes_accessed=1024, transcendentals=0),
        name="project",
    )(half, *operands, *[weight] * len(parts))


def gathered(kv_ref, list_ref, tile, group, half):
    parts = []
    for j in range(GROUP):
        row = pl.multiple_of(list_ref[tile, group * GROUP + j] * TILE, TILE)
        parts.append(kv_ref[pl.ds(row, TILE), half * HD : half * HD + HD])
    return jnp.concatenate(parts, axis=0)


def query_rows(tile):
    return pl.ds(pl.multiple_of(tile * TILE, TILE), TILE)


def score_tile(tile, groups, list_ref, count_ref, q_ref, kv_ref):
    q = q_ref[query_rows(tile), :]
    lane = lax.broadcasted_iota(jnp.int32, (TILE, GROUP * TILE), 1)
    out = []
    for g in range(groups):
        s = lax.dot_general(
            q, gathered(kv_ref, list_ref, tile, g, 0), (((1,), (1,)), ((), ())),
            preferred_element_type=jnp.float32,
        )
        out.append(jnp.where(lane < (count_ref[tile] - GROUP * g) * TILE, s, NEGATIVE))
    return out


def highest_of(scores):
    parts = [s[:, k : k + HD] for s in scores for k in range(0, GROUP * TILE, HD)]
    return jnp.max(functools.reduce(jnp.maximum, parts), axis=-1, keepdims=True)


def context_tile(tile, scores, highest, list_ref, kv_ref, o_ref):
    totals = summed = 0.0
    for g, s in enumerate(scores):
        weights = jnp.exp2((s - highest) * EXPONENT)
        for k in range(0, GROUP * TILE, HD):
            totals = totals + weights[:, k : k + HD]
        summed = summed + jnp.dot(
            weights.astype(jnp.bfloat16), gathered(kv_ref, list_ref, tile, g, 1),
            preferred_element_type=jnp.float32,
        )
    totals = jnp.sum(totals, axis=-1, keepdims=True)
    o_ref[query_rows(tile), :] = (summed / totals).astype(jnp.bfloat16)


def attend_kernel(list_ref, count_ref, order_ref, qm_ref, qp_ref, *rest):
    pieces, rest = rest[:16], rest[16:]
    outs, (kv_ref, q_ref, o_ref, sems) = rest[: 2 * CHUNKS], rest[2 * CHUNKS :]
    rows = pieces[0].shape[0]
    copies = [
        pltpu.make_async_copy(piece, kv_ref.at[pl.ds(k * rows, rows)], sems.at[k])
        for k, piece in enumerate(pieces)
    ]
    for copy in copies:
        copy.start()
    q_ref[:rows, :] = qm_ref[...]
    q_ref[rows:, :] = qp_ref[...]
    for copy in copies:
        copy.wait()
    tiles = q_ref.shape[0] // TILE

    @pl.loop(0, tiles // ROWS)
    def _(block):
        ids = [order_ref[block * ROWS + j] for j in range(ROWS)]
        longest = functools.reduce(jnp.maximum, [count_ref[t] for t in ids])
        needed = (longest + GROUP - 1) // GROUP
        for groups in range(1, SEL // GROUP + 1):

            @pl.when(needed == groups)
            def _():
                scores = [score_tile(t, groups, list_ref, count_ref, q_ref, kv_ref) for t in ids]
                tops = [highest_of(s) for s in scores]
                for t, s, top in zip(ids, scores, tops):
                    context_tile(t, s, top, list_ref, kv_ref, o_ref)


    part = outs[0].shape[0]
    for k, out in enumerate(outs):
        out[...] = o_ref[k * part : (k + 1) * part, :]


def attend(lists, counts, order, qm, qp, pieces):
    rows = qm.shape[0]
    part = jax.ShapeDtypeStruct((rows // CHUNKS, HD), jnp.bfloat16)
    return pl.pallas_call(
        attend_kernel,
        out_shape=[part] * (2 * CHUNKS),
        in_specs=[SM, SM, SM, VM, VM, HBM] + [ANY] * 15,
        out_specs=[VM] * (2 * CHUNKS),
        scratch_shapes=[
            pltpu.VMEM((16 * rows, 2 * HD), jnp.bfloat16),
            pltpu.VMEM((2 * rows, HD), jnp.bfloat16),
            pltpu.VMEM((2 * rows, HD), jnp.bfloat16),
            pltpu.SemaphoreType.DMA((16,)),
        ],
        compiler_params=pltpu.CompilerParams(vmem_limit_bytes=ATTEND_VMEM),
        cost_estimate=pl.CostEstimate(
            flops=4 * 2 * rows * SEL * TILE * HD, bytes_accessed=10 * 2**20,
            transcendentals=2 * rows * SEL * TILE,
        ),
        name="attend",
    )(lists, counts, order, qm, qp, *pieces)


def pack_kernel(spot_ref, own_ref, other_ref, own_out, other_out):
    own_out[...] = own_ref[...]
    other_out[...] = other_ref[...]


def pack_weight(spot, weight):
    rows = weight.shape[0]

    def part(flip):
        def place(r, i, spot):
            step = jnp.where(i == 2, 3, jnp.where(i == 3, 2, i))
            return r ^ spot[2], (spot[0] + step) % 4 * 2 + (spot[1] ^ flip)

        return pl.BlockSpec((HD, 256), place)

    out = pl.BlockSpec((HD, 256), lambda r, i, spot: (r, i))
    return pl.pallas_call(
        pack_kernel,
        grid_spec=pltpu.PrefetchScalarGridSpec(
            num_scalar_prefetch=1,
            grid=(rows // HD, 4),
            in_specs=[part(0), part(1)],
            out_specs=[out, out],
        ),
        out_shape=[jax.ShapeDtypeStruct((rows, 1024), weight.dtype)] * 2,
        compiler_params=pltpu.CompilerParams(vmem_limit_bytes=OUT_VMEM),
        cost_estimate=pl.CostEstimate(flops=1024, bytes_accessed=1024, transcendentals=0),
        name="pack_weight",
    )(spot, weight, weight)


def out_kernel(c0, c1, c2, c3, upper_ref, lower_ref, own_ref, *outs):
    context = jnp.concatenate([c0[...], c1[...], c2[...], c3[...]], axis=1)
    weight = jnp.concatenate([upper_ref[...], lower_ref[...]], axis=0)
    own_ref[...] = jnp.dot(context, weight[:, :256], preferred_element_type=jnp.float32)
    for k, out in enumerate(outs):
        part = weight[:, 256 * (k + 1) : 256 * (k + 2)]
        out[...] = jnp.dot(context, part, preferred_element_type=jnp.float32).astype(out.dtype)


def out_project(contexts, weights):
    rows = contexts[0].shape[0]
    return pl.pallas_call(
        out_kernel,
        in_specs=[VM] * 6,
        out_specs=[VM] * 4,
        out_shape=[jax.ShapeDtypeStruct((rows, 256), jnp.float32)]
        + [jax.ShapeDtypeStruct((rows, 256), jnp.bfloat16)] * 3,
        compiler_params=pltpu.CompilerParams(vmem_limit_bytes=OUT_VMEM),
        cost_estimate=pl.CostEstimate(
            flops=2 * rows * 512 * 1024, bytes_accessed=3 * 2**20, transcendentals=0
        ),
        name="out_project",
    )(*contexts, *weights)


def sum_kernel(*refs):
    own_ref, blocks, out_ref = refs[0], refs[1:4], refs[-1]
    total = own_ref[...]
    for block in blocks:
        total = total + block[...].astype(jnp.float32)
    out_ref[...] = total.astype(out_ref.dtype)


def sum_part(own, blocks, part, before):
    rows, columns = own.shape
    whole = pl.BlockSpec((rows, columns), lambda i: (0, 0))
    return pl.pallas_call(
        sum_kernel,
        grid=(1,),
        in_specs=[whole] * 4 + [ANY] * len(before),
        out_specs=pl.BlockSpec((rows, columns), lambda i: (part, 0)),
        out_shape=jax.ShapeDtypeStruct((rows * CHUNKS, columns), jnp.bfloat16),
        input_output_aliases={4: 0} if before else {},
        compiler_params=pltpu.CompilerParams(vmem_limit_bytes=OUT_VMEM),
        name="sum_part",
    )(own, *blocks, *before)


def place_lists(tile, counts, yl, z, core):
    per_slab = tile.shape[0] // 2
    slab = tile // per_slab
    place = (((slab % 8 // 2 - z) % 4) * 2 + ((slab // 8) ^ yl)) * 2 + ((slab % 2) ^ core)
    lists = place * per_slab + tile % per_slab
    ids = jnp.arange(counts.shape[0], dtype=jnp.int32)
    before = (counts[None, :] > counts[:, None]) | (
        (counts[None, :] == counts[:, None]) & (ids[None, :] < ids[:, None])
    )
    rank = jnp.sum(before.astype(jnp.int32), axis=1)
    order = jnp.sum(jnp.where(rank[None, :] == ids[:, None], ids[None, :], 0), axis=1)
    return lists, counts, order


def per_device(hidden_states, norm_gain, qkv_weight, out_weight, selected_tiles, selected_count):
    rows_here = selected_tiles.shape[0]
    seq = lax.axis_index("seq")
    head = lax.axis_index("head")
    yl, z, core = seq // 8, (seq % 8) // 2, seq % 2
    yh = head % 2

    x = head // 2
    spot = jnp.stack([x, yh, yl]).astype(jnp.int32)
    own_weight, sent_weight = pack_weight(spot, out_weight)

    barrier = lax.optimization_barrier
    half = jnp.reshape(yl, (1,)).astype(jnp.int32)
    gain = norm_gain.reshape(1, -1)
    kvo, kvm = project(
        keys_kernel, (hidden_states, gain), qkv_weight, half,
        ((1, 1), (2, 1), (1, 0), (2, 0)), (2 * HD, 2 * HD), 60 * 2**20,
    )
    qm, qo = project(
        queries_kernel, (hidden_states, gain), qkv_weight, half,
        ((0, 0), (0, 1)), (HD, HD), 24 * 2**20,
    )

    kvp = move(kvo, dyl=1)
    first, kvo = barrier((selected_count, kvo))
    kvm, first = barrier((kvm, move(first, dc=1)))
    up_m, down_m = move(kvm, dz=1), move(kvm, dz=-1)
    kvp, sent_weight, first = barrier((kvp, sent_weight, first))
    up_p, down_p = move(kvp, dz=1), move(kvp, dz=-1)
    other_weight = move(sent_weight, dyh=1)
    core_up_m, core_down_m = move(up_m, dc=1), move(down_m, dc=1)
    counts = jnp.maximum(selected_count, jnp.minimum(first, 1))
    packed = jnp.concatenate(
        [selected_tiles, counts[:, None], jnp.zeros((rows_here, 95), jnp.int32)], axis=1
    )
    up_m, down_m, up_p, down_p, qo, packed, core_up_m, core_down_m, other_weight = barrier(
        (up_m, down_m, up_p, down_p, qo, packed, core_up_m, core_down_m, other_weight)
    )
    far_m, far_p = move(up_m, dz=1), move(down_p, dz=-1)
    qp, packed_p = move(qo, dyl=1), move(packed, dyl=1)
    qp, packed_p, up_p, down_p, own_m, own_p = barrier((qp, packed_p, up_p, down_p, kvm, kvp))
    core_m, core_p = move(own_m, dc=1), move(own_p, dc=1)
    core_up_p, core_down_p = move(up_p, dc=1), move(down_p, dc=1)
    packed = jnp.concatenate([packed, packed_p], axis=0)
    lists, counts, order = place_lists(packed[:, :SEL], packed[:, SEL], yl, z, core)
    far_m, far_p, core_m, core_p, core_up_p, core_down_p, lists, counts, order = barrier(
        (far_m, far_p, core_m, core_p, core_up_p, core_down_p, lists, counts, order)
    )
    core_far_m, core_far_p = move(far_m, dc=1), move(far_p, dc=1)
    parts = attend(
        lists, counts, order, qm, qp,
        (kvm, core_m, kvp, core_p, down_m, core_down_m, down_p, core_down_p,
         far_m, core_far_m, far_p, core_far_p, up_m, core_up_m, up_p, core_up_p),
    )

    weights = (own_weight, other_weight)
    before = ()
    for k, (mine, partner) in enumerate(zip(parts[:CHUNKS], parts[CHUNKS:])):
        contexts = (
            mine, move(partner, dyl=1), move(mine, dyh=1), move(partner, dyl=1, dyh=1)
        )
        own, *sent = out_project(contexts, weights)
        blocks = [move(block, dx=d) for d, block in zip((1, 3, 2), sent)]
        before = (sum_part(own, blocks, k, before),)
    return before[0]


def solution(mesh):
    return jax.shard_map(
        per_device,
        mesh=mesh,
        in_specs=(
            P("seq", None),
            P(),
            P(None, None, "head"),
            P("head", None),
            P("seq", None),
            P("seq"),
        ),
        out_specs=P("seq", "head"),
        check_vma=False,
    )
```

```python
import functools

import jax
import jax.numpy as jnp
from jax import lax
from jax.experimental import pallas as pl
from jax.experimental.pallas import tpu as pltpu
from jax.sharding import PartitionSpec as P

D = 2048
HD = 128
TILE = 64
SEL = 32
EPSILON = 1e-06
NEGATIVE = -1e30
EXPONENT = float(HD**-0.5 * 1.4426950408889634)
AXES = ("seq", "head")
GROUP = 4
ROWS = 8
VM = pl.BlockSpec(memory_space=pltpu.VMEM)
SM = pl.BlockSpec(memory_space=pltpu.SMEM)
ANY = pl.BlockSpec(memory_space=pl.ANY)
HBM = pl.BlockSpec(memory_space=pltpu.HBM)
ATTEND_VMEM = 24 * 2**20
OUT_VMEM = 12 * 2**20
CHUNKS = 2


def coords(i):
    s, h = divmod(i, 8)
    yl, r = divmod(s, 8)
    z, c = divmod(r, 2)
    x, yh = divmod(h, 2)
    return x, yh, yl, z, c


def index(x, yh, yl, z, c):
    return ((yl * 4 + z) * 2 + c) * 8 + x * 2 + yh


def move(array, dx=0, dyh=0, dyl=0, dz=0, dc=0):
    pairs = []
    for i in range(128):
        x, yh, yl, z, c = coords(i)
        pairs.append((i, index((x + dx) % 4, yh ^ dyh, yl ^ dyl, (z + dz) % 4, c ^ dc)))
    return lax.ppermute(array, AXES, pairs)


def normalize(h_ref, gain_ref):
    values = h_ref[...].astype(jnp.float32)
    spread = jnp.mean(values * values, axis=-1, keepdims=True)
    return (values * lax.rsqrt(spread + EPSILON) * gain_ref[...]).astype(jnp.bfloat16)


def keys_kernel(half_ref, h_ref, gain_ref, ko, vo, km, vm, kvo_ref, kvm_ref):
    normed = normalize(h_ref, gain_ref)
    for k_ref, v_ref, out_ref in ((ko, vo, kvo_ref), (km, vm, kvm_ref)):
        weight = jnp.concatenate([k_ref[0], v_ref[0]], axis=1)
        both = jnp.dot(normed, weight, preferred_element_type=jnp.float32)
        out_ref[...] = both.astype(jnp.bfloat16)


def queries_kernel(half_ref, h_ref, gain_ref, qm, qo, qm_ref, qo_ref):
    weight = jnp.concatenate([qm[0], qo[0]], axis=1)
    both = jnp.dot(normalize(h_ref, gain_ref), weight, preferred_element_type=jnp.float32)
    both = both.astype(jnp.bfloat16)
    qm_ref[...] = both[:, :HD]
    qo_ref[...] = both[:, HD:]


def project(kernel, operands, weight, half, parts, outs, vmem):
    rows, width = operands[0].shape
    block = 512

    def part(member, flip):
        return pl.BlockSpec((1, width, HD), lambda i, half: (member, 0, half[0] ^ flip))

    def rows_of(n):
        return pl.BlockSpec((block, n), lambda i, half: (i, 0))

    return pl.pallas_call(
        kernel,
        grid_spec=pltpu.PrefetchScalarGridSpec(
            num_scalar_prefetch=1,
            grid=(rows // block,),
            in_specs=[rows_of(width)]
            + [pl.BlockSpec((1, width), lambda i, half: (0, 0))] * (len(operands) - 1)
            + [part(*p) for p in parts],
            out_specs=[rows_of(n) for n in outs],
        ),
        out_shape=[jax.ShapeDtypeStruct((rows, n), jnp.bfloat16) for n in outs],
        compiler_params=pltpu.CompilerParams(vmem_limit_bytes=vmem),
        cost_estimate=pl.CostEstimate(flops=1024, bytes_accessed=1024, transcendentals=0),
        name="project",
    )(half, *operands, *[weight] * len(parts))


def gathered(kv_ref, list_ref, tile, group, half):
    parts = []
    for j in range(GROUP):
        row = pl.multiple_of(list_ref[tile, group * GROUP + j] * TILE, TILE)
        parts.append(kv_ref[pl.ds(row, TILE), half * HD : half * HD + HD])
    return jnp.concatenate(parts, axis=0)


def query_rows(tile):
    return pl.ds(pl.multiple_of(tile * TILE, TILE), TILE)


def score_tile(tile, groups, list_ref, count_ref, q_ref, kv_ref):
    q = q_ref[query_rows(tile), :]
    lane = lax.broadcasted_iota(jnp.int32, (TILE, GROUP * TILE), 1)
    out = []
    for g in range(groups):
        s = lax.dot_general(
            q, gathered(kv_ref, list_ref, tile, g, 0), (((1,), (1,)), ((), ())),
            preferred_element_type=jnp.float32,
        )
        out.append(jnp.where(lane < (count_ref[tile] - GROUP * g) * TILE, s, NEGATIVE))
    return out


def highest_of(scores):
    parts = [s[:, k : k + HD] for s in scores for k in range(0, GROUP * TILE, HD)]
    return jnp.max(functools.reduce(jnp.maximum, parts), axis=-1, keepdims=True)


def context_tile(tile, scores, highest, list_ref, kv_ref, o_ref):
    totals = summed = 0.0
    for g, s in enumerate(scores):
        weights = jnp.exp2((s - highest) * EXPONENT)
        for k in range(0, GROUP * TILE, HD):
            totals = totals + weights[:, k : k + HD]
        summed = summed + jnp.dot(
            weights.astype(jnp.bfloat16), gathered(kv_ref, list_ref, tile, g, 1),
            preferred_element_type=jnp.float32,
        )
    totals = jnp.sum(totals, axis=-1, keepdims=True)
    o_ref[query_rows(tile), :] = (summed / totals).astype(jnp.bfloat16)


def attend_kernel(list_ref, count_ref, order_ref, qm_ref, qp_ref, *rest):
    pieces, rest = rest[:16], rest[16:]
    outs, (kv_ref, q_ref, o_ref, sems) = rest[: 2 * CHUNKS], rest[2 * CHUNKS :]
    rows = pieces[0].shape[0]
    copies = [
        pltpu.make_async_copy(piece, kv_ref.at[pl.ds(k * rows, rows)], sems.at[k])
        for k, piece in enumerate(pieces)
    ]
    for copy in copies:
        copy.start()
    q_ref[:rows, :] = qm_ref[...]
    q_ref[rows:, :] = qp_ref[...]
    for copy in copies:
        copy.wait()
    tiles = q_ref.shape[0] // TILE

    @pl.loop(0, tiles // ROWS)
    def _(block):
        ids = [order_ref[block * ROWS + j] for j in range(ROWS)]
        longest = functools.reduce(jnp.maximum, [count_ref[t] for t in ids])
        needed = (longest + GROUP - 1) // GROUP
        for groups in range(1, SEL // GROUP + 1):

            @pl.when(needed == groups)
            def _():
                scores = [score_tile(t, groups, list_ref, count_ref, q_ref, kv_ref) for t in ids]
                tops = [highest_of(s) for s in scores]
                for t, s, top in zip(ids, scores, tops):
                    context_tile(t, s, top, list_ref, kv_ref, o_ref)


    part = outs[0].shape[0]
    for k, out in enumerate(outs):
        out[...] = o_ref[k * part : (k + 1) * part, :]


def attend(lists, counts, order, qm, qp, pieces):
    rows = qm.shape[0]
    part = jax.ShapeDtypeStruct((rows // CHUNKS, HD), jnp.bfloat16)
    return pl.pallas_call(
        attend_kernel,
        out_shape=[part] * (2 * CHUNKS),
        in_specs=[SM, SM, SM, VM, VM, HBM] + [ANY] * 15,
        out_specs=[VM] * (2 * CHUNKS),
        scratch_shapes=[
            pltpu.VMEM((16 * rows, 2 * HD), jnp.bfloat16),
            pltpu.VMEM((2 * rows, HD), jnp.bfloat16),
            pltpu.VMEM((2 * rows, HD), jnp.bfloat16),
            pltpu.SemaphoreType.DMA((16,)),
        ],
        compiler_params=pltpu.CompilerParams(vmem_limit_bytes=ATTEND_VMEM),
        cost_estimate=pl.CostEstimate(
            flops=4 * 2 * rows * SEL * TILE * HD, bytes_accessed=10 * 2**20,
            transcendentals=2 * rows * SEL * TILE,
        ),
        name="attend",
    )(lists, counts, order, qm, qp, *pieces)


def pack_weight(spot, weight, flip, held=None):
    rows = weight.shape[0]

    def kernel(spot_ref, weight_ref, *refs):
        out_ref = refs[-1]
        x, yh, yl = spot_ref[0], spot_ref[1], spot_ref[2]
        for i, d in enumerate((0, 1, 3, 2)):
            start = ((x + d) % 4 * 2 + (yh ^ flip)) * 256
            columns = pl.ds(pl.multiple_of(start, 256), 256)
            for r in range(rows // HD):
                taken = pl.ds(pl.multiple_of((r ^ yl) * HD, HD), HD)
                out_ref[r * HD : (r + 1) * HD, i * 256 : (i + 1) * 256] = weight_ref[taken, columns]
        if held is not None:
            out_ref[rows:, :] = refs[0][...]

    extra = [] if held is None else [held]
    return pl.pallas_call(
        kernel,
        in_specs=[SM] + [VM] * (1 + len(extra)),
        out_specs=VM,
        out_shape=jax.ShapeDtypeStruct((rows * (1 + len(extra)), 1024), weight.dtype),
        compiler_params=pltpu.CompilerParams(vmem_limit_bytes=OUT_VMEM),
        cost_estimate=pl.CostEstimate(flops=1024, bytes_accessed=1024, transcendentals=0),
        name="pack_weight",
    )(spot, weight, *extra)


def out_kernel(c0, c1, c2, c3, weight_ref, own_ref, *outs):
    context = jnp.concatenate([c0[...], c1[...], c2[...], c3[...]], axis=1)
    weight = weight_ref[...]
    own_ref[...] = jnp.dot(context, weight[:, :256], preferred_element_type=jnp.float32)
    for k, out in enumerate(outs):
        part = weight[:, 256 * (k + 1) : 256 * (k + 2)]
        out[...] = jnp.dot(context, part, preferred_element_type=jnp.float32).astype(out.dtype)


def out_project(contexts, weight):
    rows = contexts[0].shape[0]
    return pl.pallas_call(
        out_kernel,
        in_specs=[VM] * 5,
        out_specs=[VM] * 4,
        out_shape=[jax.ShapeDtypeStruct((rows, 256), jnp.float32)]
        + [jax.ShapeDtypeStruct((rows, 256), jnp.bfloat16)] * 3,
        compiler_params=pltpu.CompilerParams(vmem_limit_bytes=OUT_VMEM),
        cost_estimate=pl.CostEstimate(
            flops=2 * rows * 512 * 1024, bytes_accessed=3 * 2**20, transcendentals=0
        ),
        name="out_project",
    )(*contexts, weight)


def sum_kernel(*refs):
    own_ref, blocks, out_ref = refs[0], refs[1:4], refs[-1]
    total = own_ref[...]
    for block in blocks:
        total = total + block[...].astype(jnp.float32)
    out_ref[...] = total.astype(out_ref.dtype)


def sum_part(own, blocks, part, before):
    rows, columns = own.shape
    whole = pl.BlockSpec((rows, columns), lambda i: (0, 0))
    return pl.pallas_call(
        sum_kernel,
        grid=(1,),
        in_specs=[whole] * 4 + [ANY] * len(before),
        out_specs=pl.BlockSpec((rows, columns), lambda i: (part, 0)),
        out_shape=jax.ShapeDtypeStruct((rows * CHUNKS, columns), jnp.bfloat16),
        input_output_aliases={4: 0} if before else {},
        compiler_params=pltpu.CompilerParams(vmem_limit_bytes=OUT_VMEM),
        name="sum_part",
    )(own, *blocks, *before)


def place_lists(tile, counts, yl, z, core):
    per_slab = tile.shape[0] // 2
    slab = tile // per_slab
    place = (((slab % 8 // 2 - z) % 4) * 2 + ((slab // 8) ^ yl)) * 2 + ((slab % 2) ^ core)
    lists = place * per_slab + tile % per_slab
    ids = jnp.arange(counts.shape[0], dtype=jnp.int32)
    before = (counts[None, :] > counts[:, None]) | (
        (counts[None, :] == counts[:, None]) & (ids[None, :] < ids[:, None])
    )
    rank = jnp.sum(before.astype(jnp.int32), axis=1)
    order = jnp.sum(jnp.where(rank[None, :] == ids[:, None], ids[None, :], 0), axis=1)
    return lists, counts, order


def per_device(hidden_states, norm_gain, qkv_weight, out_weight, selected_tiles, selected_count):
    rows_here = selected_tiles.shape[0]
    seq = lax.axis_index("seq")
    head = lax.axis_index("head")
    yl, z, core = seq // 8, (seq % 8) // 2, seq % 2
    yh = head % 2

    x = head // 2
    spot = jnp.stack([x, yh, yl]).astype(jnp.int32)
    sent_weight = pack_weight(spot, out_weight, 1)

    barrier = lax.optimization_barrier
    half = jnp.reshape(yl, (1,)).astype(jnp.int32)
    gain = norm_gain.reshape(1, -1)
    kvo, kvm = project(
        keys_kernel, (hidden_states, gain), qkv_weight, half,
        ((1, 1), (2, 1), (1, 0), (2, 0)), (2 * HD, 2 * HD), 60 * 2**20,
    )
    qm, qo = project(
        queries_kernel, (hidden_states, gain), qkv_weight, half,
        ((0, 0), (0, 1)), (HD, HD), 24 * 2**20,
    )

    kvp = move(kvo, dyl=1)
    first, kvo = barrier((selected_count, kvo))
    kvm, first = barrier((kvm, move(first, dc=1)))
    up_m, down_m = move(kvm, dz=1), move(kvm, dz=-1)
    kvp, sent_weight, first = barrier((kvp, sent_weight, first))
    up_p, down_p = move(kvp, dz=1), move(kvp, dz=-1)
    other_weight = move(sent_weight, dyh=1)
    core_up_m, core_down_m = move(up_m, dc=1), move(down_m, dc=1)
    counts = jnp.maximum(selected_count, jnp.minimum(first, 1))
    packed = jnp.concatenate(
        [selected_tiles, counts[:, None], jnp.zeros((rows_here, 95), jnp.int32)], axis=1
    )
    up_m, down_m, up_p, down_p, qo, packed, core_up_m, core_down_m, other_weight = barrier(
        (up_m, down_m, up_p, down_p, qo, packed, core_up_m, core_down_m, other_weight)
    )
    far_m, far_p = move(up_m, dz=1), move(down_p, dz=-1)
    qp, packed_p = move(qo, dyl=1), move(packed, dyl=1)
    qp, packed_p, up_p, down_p, own_m, own_p = barrier((qp, packed_p, up_p, down_p, kvm, kvp))
    core_m, core_p = move(own_m, dc=1), move(own_p, dc=1)
    core_up_p, core_down_p = move(up_p, dc=1), move(down_p, dc=1)
    packed = jnp.concatenate([packed, packed_p], axis=0)
    lists, counts, order = place_lists(packed[:, :SEL], packed[:, SEL], yl, z, core)
    far_m, far_p, core_m, core_p, core_up_p, core_down_p, lists, counts, order = barrier(
        (far_m, far_p, core_m, core_p, core_up_p, core_down_p, lists, counts, order)
    )
    core_far_m, core_far_p = move(far_m, dc=1), move(far_p, dc=1)
    parts = attend(
        lists, counts, order, qm, qp,
        (kvm, core_m, kvp, core_p, down_m, core_down_m, down_p, core_down_p,
         far_m, core_far_m, far_p, core_far_p, up_m, core_up_m, up_p, core_up_p),
    )

    *parts, out_weight = barrier((*parts, out_weight))
    weight = pack_weight(spot, out_weight, 0, other_weight)
    before = ()
    for k, (mine, partner) in enumerate(zip(parts[:CHUNKS], parts[CHUNKS:])):
        contexts = (
            mine, move(partner, dyl=1), move(mine, dyh=1), move(partner, dyl=1, dyh=1)
        )
        own, *sent = out_project(contexts, weight)
        blocks = [move(block, dx=d) for d, block in zip((1, 3, 2), sent)]
        before = (sum_part(own, blocks, k, before),)
    return before[0]


def solution(mesh):
    return jax.shard_map(
        per_device,
        mesh=mesh,
        in_specs=(
            P("seq", None),
            P(),
            P(None, None, "head"),
            P("head", None),
            P("seq", None),
            P("seq"),
        ),
        out_specs=P("seq", "head"),
        check_vma=False,
    )
```

```python
import functools

import jax
import jax.numpy as jnp
from jax import lax
from jax.experimental import pallas as pl
from jax.experimental.pallas import tpu as pltpu
from jax.sharding import PartitionSpec as P

D = 2048
HD = 128
TILE = 64
SEL = 32
EPSILON = 1e-06
NEGATIVE = -1e30
EXPONENT = float(HD**-0.5 * 1.4426950408889634)
AXES = ("seq", "head")
GROUP = 4
ROWS = 8
VM = pl.BlockSpec(memory_space=pltpu.VMEM)
SM = pl.BlockSpec(memory_space=pltpu.SMEM)
ANY = pl.BlockSpec(memory_space=pl.ANY)
HBM = pl.BlockSpec(memory_space=pltpu.HBM)
ATTEND_VMEM = 24 * 2**20
OUT_VMEM = 12 * 2**20
CHUNKS = 2


def coords(i):
    s, h = divmod(i, 8)
    yl, r = divmod(s, 8)
    z, c = divmod(r, 2)
    x, yh = divmod(h, 2)
    return x, yh, yl, z, c


def index(x, yh, yl, z, c):
    return ((yl * 4 + z) * 2 + c) * 8 + x * 2 + yh


def move(array, dx=0, dyh=0, dyl=0, dz=0, dc=0):
    pairs = []
    for i in range(128):
        x, yh, yl, z, c = coords(i)
        pairs.append((i, index((x + dx) % 4, yh ^ dyh, yl ^ dyl, (z + dz) % 4, c ^ dc)))
    return lax.ppermute(array, AXES, pairs)


def normalize(h_ref, gain_ref):
    values = h_ref[...].astype(jnp.float32)
    spread = jnp.mean(values * values, axis=-1, keepdims=True)
    return (values * lax.rsqrt(spread + EPSILON) * gain_ref[...]).astype(jnp.bfloat16)


def keys_kernel(half_ref, h_ref, gain_ref, ko, vo, km, vm, kvo_ref, kvm_ref):
    normed = normalize(h_ref, gain_ref)
    for k_ref, v_ref, out_ref in ((ko, vo, kvo_ref), (km, vm, kvm_ref)):
        weight = jnp.concatenate([k_ref[0], v_ref[0]], axis=1)
        both = jnp.dot(normed, weight, preferred_element_type=jnp.float32)
        out_ref[...] = both.astype(jnp.bfloat16)


def queries_kernel(half_ref, h_ref, gain_ref, qm, qo, qm_ref, qo_ref):
    weight = jnp.concatenate([qm[0], qo[0]], axis=1)
    both = jnp.dot(normalize(h_ref, gain_ref), weight, preferred_element_type=jnp.float32)
    both = both.astype(jnp.bfloat16)
    qm_ref[...] = both[:, :HD]
    qo_ref[...] = both[:, HD:]


def project(kernel, operands, weight, half, parts, outs, vmem):
    rows, width = operands[0].shape
    block = 512

    def part(member, flip):
        return pl.BlockSpec((1, width, HD), lambda i, half: (member, 0, half[0] ^ flip))

    def rows_of(n):
        return pl.BlockSpec((block, n), lambda i, half: (i, 0))

    return pl.pallas_call(
        kernel,
        grid_spec=pltpu.PrefetchScalarGridSpec(
            num_scalar_prefetch=1,
            grid=(rows // block,),
            in_specs=[rows_of(width)]
            + [pl.BlockSpec((1, width), lambda i, half: (0, 0))] * (len(operands) - 1)
            + [part(*p) for p in parts],
            out_specs=[rows_of(n) for n in outs],
        ),
        out_shape=[jax.ShapeDtypeStruct((rows, n), jnp.bfloat16) for n in outs],
        compiler_params=pltpu.CompilerParams(vmem_limit_bytes=vmem),
        cost_estimate=pl.CostEstimate(flops=1024, bytes_accessed=1024, transcendentals=0),
        name="project",
    )(half, *operands, *[weight] * len(parts))


def gathered(kv_ref, list_ref, tile, group, half):
    parts = []
    for j in range(GROUP):
        row = pl.multiple_of(list_ref[tile, group * GROUP + j] * TILE, TILE)
        parts.append(kv_ref[pl.ds(row, TILE), half * HD : half * HD + HD])
    return jnp.concatenate(parts, axis=0)


def query_rows(tile):
    return pl.ds(pl.multiple_of(tile * TILE, TILE), TILE)


def score_tile(tile, groups, list_ref, count_ref, q_ref, kv_ref):
    q = q_ref[query_rows(tile), :]
    lane = lax.broadcasted_iota(jnp.int32, (TILE, GROUP * TILE), 1)
    out = []
    for g in range(groups):
        s = lax.dot_general(
            q, gathered(kv_ref, list_ref, tile, g, 0), (((1,), (1,)), ((), ())),
            preferred_element_type=jnp.float32,
        )
        out.append(jnp.where(lane < (count_ref[tile] - GROUP * g) * TILE, s, NEGATIVE))
    return out


def highest_of(scores):
    parts = [s[:, k : k + HD] for s in scores for k in range(0, GROUP * TILE, HD)]
    return jnp.max(functools.reduce(jnp.maximum, parts), axis=-1, keepdims=True)


def context_tile(tile, scores, highest, list_ref, kv_ref, o_ref):
    totals = summed = 0.0
    for g, s in enumerate(scores):
        weights = jnp.exp2((s - highest) * EXPONENT)
        for k in range(0, GROUP * TILE, HD):
            totals = totals + weights[:, k : k + HD]
        summed = summed + jnp.dot(
            weights.astype(jnp.bfloat16), gathered(kv_ref, list_ref, tile, g, 1),
            preferred_element_type=jnp.float32,
        )
    totals = jnp.sum(totals, axis=-1, keepdims=True)
    o_ref[query_rows(tile), :] = (summed / totals).astype(jnp.bfloat16)


def attend_kernel(list_ref, count_ref, order_ref, qm_ref, qp_ref, *rest):
    pieces, rest = rest[:16], rest[16:]
    outs, (kv_ref, q_ref, o_ref, sems) = rest[: 2 * CHUNKS], rest[2 * CHUNKS :]
    rows = pieces[0].shape[0]
    copies = [
        pltpu.make_async_copy(piece, kv_ref.at[pl.ds(k * rows, rows)], sems.at[k])
        for k, piece in enumerate(pieces)
    ]
    for copy in copies:
        copy.start()
    q_ref[:rows, :] = qm_ref[...]
    q_ref[rows:, :] = qp_ref[...]
    for copy in copies:
        copy.wait()
    tiles = q_ref.shape[0] // TILE

    @pl.loop(0, tiles // ROWS)
    def _(block):
        ids = [order_ref[block * ROWS + j] for j in range(ROWS)]
        longest = functools.reduce(jnp.maximum, [count_ref[t] for t in ids])
        needed = (longest + GROUP - 1) // GROUP
        for groups in range(1, SEL // GROUP + 1):

            @pl.when(needed == groups)
            def _():
                scores = [score_tile(t, groups, list_ref, count_ref, q_ref, kv_ref) for t in ids]
                tops = [highest_of(s) for s in scores]
                for t, s, top in zip(ids, scores, tops):
                    context_tile(t, s, top, list_ref, kv_ref, o_ref)


    part = outs[0].shape[0]
    for k, out in enumerate(outs):
        out[...] = o_ref[k * part : (k + 1) * part, :]


def attend(lists, counts, order, qm, qp, pieces):
    rows = qm.shape[0]
    part = jax.ShapeDtypeStruct((rows // CHUNKS, HD), jnp.bfloat16)
    return pl.pallas_call(
        attend_kernel,
        out_shape=[part] * (2 * CHUNKS),
        in_specs=[SM, SM, SM, VM, VM, HBM] + [ANY] * 15,
        out_specs=[VM] * (2 * CHUNKS),
        scratch_shapes=[
            pltpu.VMEM((16 * rows, 2 * HD), jnp.bfloat16),
            pltpu.VMEM((2 * rows, HD), jnp.bfloat16),
            pltpu.VMEM((2 * rows, HD), jnp.bfloat16),
            pltpu.SemaphoreType.DMA((16,)),
        ],
        compiler_params=pltpu.CompilerParams(vmem_limit_bytes=ATTEND_VMEM),
        cost_estimate=pl.CostEstimate(
            flops=4 * 2 * rows * SEL * TILE * HD, bytes_accessed=10 * 2**20,
            transcendentals=2 * rows * SEL * TILE,
        ),
        name="attend",
    )(lists, counts, order, qm, qp, *pieces)


def pack_weight(spot, weight, flip, held=None):
    rows = weight.shape[0]

    def kernel(spot_ref, weight_ref, *refs):
        out_ref = refs[-1]
        x, yh, yl = spot_ref[0], spot_ref[1], spot_ref[2]
        for i, d in enumerate((0, 1, 3, 2)):
            start = ((x + d) % 4 * 2 + (yh ^ flip)) * 256
            columns = pl.ds(pl.multiple_of(start, 256), 256)
            for r in range(rows // HD):
                taken = pl.ds(pl.multiple_of((r ^ yl) * HD, HD), HD)
                out_ref[r * HD : (r + 1) * HD, i * 256 : (i + 1) * 256] = weight_ref[taken, columns]
        if held is not None:
            out_ref[rows:, :] = refs[0][...]

    extra = [] if held is None else [held]
    return pl.pallas_call(
        kernel,
        in_specs=[SM] + [VM] * (1 + len(extra)),
        out_specs=VM,
        out_shape=jax.ShapeDtypeStruct((rows * (1 + len(extra)), 1024), weight.dtype),
        compiler_params=pltpu.CompilerParams(vmem_limit_bytes=OUT_VMEM),
        cost_estimate=pl.CostEstimate(flops=1024, bytes_accessed=1024, transcendentals=0),
        name="pack_weight",
    )(spot, weight, *extra)


def out_kernel(c0, c1, c2, c3, weight_ref, own_ref, plus_ref, minus_ref, up_ref, down_ref):
    context = jnp.concatenate([c0[...], c1[...], c2[...], c3[...]], axis=1)

    def product(k):
        part = weight_ref[:, 256 * k : 256 * (k + 1)]
        return jnp.dot(context, part, preferred_element_type=jnp.float32)

    far = product(3).astype(up_ref.dtype)
    half = up_ref.shape[0]
    up_ref[...] = far[:half]
    down_ref[...] = far[half:]
    for k, out in enumerate((own_ref, plus_ref, minus_ref)):
        out[...] = product(k)


def out_project(contexts, weight):
    rows = contexts[0].shape[0]
    return pl.pallas_call(
        out_kernel,
        in_specs=[VM] * 5,
        out_specs=[VM] * 5,
        out_shape=[jax.ShapeDtypeStruct((rows, 256), jnp.float32)] * 3
        + [jax.ShapeDtypeStruct((rows // 2, 256), jnp.bfloat16)] * 2,
        compiler_params=pltpu.CompilerParams(vmem_limit_bytes=OUT_VMEM),
        cost_estimate=pl.CostEstimate(
            flops=2 * rows * 512 * 1024, bytes_accessed=3 * 2**20, transcendentals=0
        ),
        name="out_project",
    )(*contexts, weight)


def sum_kernel(plus_ref, minus_ref, up_ref, down_ref, plus_out, minus_out):
    half = up_ref.shape[0]
    plus, minus = plus_ref[...], minus_ref[...]
    plus_out[:half, :] = (plus[:half] + up_ref[...].astype(jnp.float32)).astype(plus_out.dtype)
    plus_out[half:, :] = plus[half:].astype(plus_out.dtype)
    minus_out[:half, :] = minus[:half].astype(minus_out.dtype)
    lower = minus[half:] + down_ref[...].astype(jnp.float32)
    minus_out[half:, :] = lower.astype(minus_out.dtype)


def sum_blocks(plus, minus, up, down):
    return pl.pallas_call(
        sum_kernel,
        in_specs=[VM] * 4,
        out_specs=[VM] * 2,
        out_shape=[jax.ShapeDtypeStruct(plus.shape, jnp.bfloat16)] * 2,
        compiler_params=pltpu.CompilerParams(vmem_limit_bytes=OUT_VMEM),
        name="sum_blocks",
    )(plus, minus, up, down)


def finish_kernel(*refs):
    out_ref = refs[-1]
    rows = refs[0].shape[0]
    for k in range(2):
        own, *blocks = refs[3 * k : 3 * k + 3]
        total = own[...]
        for block in blocks:
            total = total + block[...].astype(jnp.float32)
        out_ref[k * rows : (k + 1) * rows, :] = total.astype(out_ref.dtype)


def finish(first, second):
    rows, columns = first[0].shape
    return pl.pallas_call(
        finish_kernel,
        in_specs=[VM] * 6,
        out_specs=VM,
        out_shape=jax.ShapeDtypeStruct((2 * rows, columns), jnp.bfloat16),
        compiler_params=pltpu.CompilerParams(vmem_limit_bytes=OUT_VMEM),
        name="finish",
    )(*first, *second)


def place_lists(tile, counts, yl, z, core):
    per_slab = tile.shape[0] // 2
    slab = tile // per_slab
    place = (((slab % 8 // 2 - z) % 4) * 2 + ((slab // 8) ^ yl)) * 2 + ((slab % 2) ^ core)
    lists = place * per_slab + tile % per_slab
    ids = jnp.arange(counts.shape[0], dtype=jnp.int32)
    before = (counts[None, :] > counts[:, None]) | (
        (counts[None, :] == counts[:, None]) & (ids[None, :] < ids[:, None])
    )
    rank = jnp.sum(before.astype(jnp.int32), axis=1)
    order = jnp.sum(jnp.where(rank[None, :] == ids[:, None], ids[None, :], 0), axis=1)
    return lists, counts, order


def per_device(hidden_states, norm_gain, qkv_weight, out_weight, selected_tiles, selected_count):
    rows_here = selected_tiles.shape[0]
    seq = lax.axis_index("seq")
    head = lax.axis_index("head")
    yl, z, core = seq // 8, (seq % 8) // 2, seq % 2
    yh = head % 2

    x = head // 2
    spot = jnp.stack([x, yh, yl]).astype(jnp.int32)
    sent_weight = pack_weight(spot, out_weight, 1)

    barrier = lax.optimization_barrier
    half = jnp.reshape(yl, (1,)).astype(jnp.int32)
    gain = norm_gain.reshape(1, -1)
    kvo, kvm = project(
        keys_kernel, (hidden_states, gain), qkv_weight, half,
        ((1, 1), (2, 1), (1, 0), (2, 0)), (2 * HD, 2 * HD), 60 * 2**20,
    )
    qm, qo = project(
        queries_kernel, (hidden_states, gain), qkv_weight, half,
        ((0, 0), (0, 1)), (HD, HD), 24 * 2**20,
    )

    kvp = move(kvo, dyl=1)
    first, kvo = barrier((selected_count, kvo))
    kvm, first = barrier((kvm, move(first, dc=1)))
    up_m, down_m = move(kvm, dz=1), move(kvm, dz=-1)
    kvp, sent_weight, first = barrier((kvp, sent_weight, first))
    up_p, down_p = move(kvp, dz=1), move(kvp, dz=-1)
    other_weight = move(sent_weight, dyh=1)
    core_up_m, core_down_m = move(up_m, dc=1), move(down_m, dc=1)
    counts = jnp.maximum(selected_count, jnp.minimum(first, 1))
    packed = jnp.concatenate(
        [selected_tiles, counts[:, None], jnp.zeros((rows_here, 95), jnp.int32)], axis=1
    )
    up_m, down_m, up_p, down_p, qo, packed, core_up_m, core_down_m, other_weight = barrier(
        (up_m, down_m, up_p, down_p, qo, packed, core_up_m, core_down_m, other_weight)
    )
    far_m, far_p = move(up_m, dz=1), move(down_p, dz=-1)
    qp, packed_p = move(qo, dyl=1), move(packed, dyl=1)
    qp, packed_p, up_p, down_p, own_m, own_p = barrier((qp, packed_p, up_p, down_p, kvm, kvp))
    core_m, core_p = move(own_m, dc=1), move(own_p, dc=1)
    core_up_p, core_down_p = move(up_p, dc=1), move(down_p, dc=1)
    packed = jnp.concatenate([packed, packed_p], axis=0)
    lists, counts, order = place_lists(packed[:, :SEL], packed[:, SEL], yl, z, core)
    far_m, far_p, core_m, core_p, core_up_p, core_down_p, lists, counts, order = barrier(
        (far_m, far_p, core_m, core_p, core_up_p, core_down_p, lists, counts, order)
    )
    core_far_m, core_far_p = move(far_m, dc=1), move(far_p, dc=1)
    parts = attend(
        lists, counts, order, qm, qp,
        (kvm, core_m, kvp, core_p, down_m, core_down_m, down_p, core_down_p,
         far_m, core_far_m, far_p, core_far_p, up_m, core_up_m, up_p, core_up_p),
    )

    *parts, out_weight = barrier((*parts, out_weight))
    weight = pack_weight(spot, out_weight, 0, other_weight)
    contexts = [
        (mine, move(partner, dyl=1), move(mine, dyh=1), move(partner, dyl=1, dyh=1))
        for mine, partner in zip(parts[:CHUNKS], parts[CHUNKS:])
    ]
    done = []
    for held in contexts:
        own, plus, minus, up, down = out_project(held, weight)
        plus, minus = sum_blocks(plus, minus, move(up, dx=1), move(down, dx=-1))
        done.append((own, move(plus, dx=1), move(minus, dx=-1)))
    return finish(*done)


def solution(mesh):
    return jax.shard_map(
        per_device,
        mesh=mesh,
        in_specs=(
            P("seq", None),
            P(),
            P(None, None, "head"),
            P("head", None),
            P("seq", None),
            P("seq"),
        ),
        out_specs=P("seq", "head"),
        check_vma=False,
    )
```

```python
import functools

import jax
import jax.numpy as jnp
from jax import lax
from jax.experimental import pallas as pl
from jax.experimental.pallas import tpu as pltpu
from jax.sharding import PartitionSpec as P

D = 2048
HD = 128
TILE = 64
SEL = 32
EPSILON = 1e-06
NEGATIVE = -1e30
EXPONENT = float(HD**-0.5 * 1.4426950408889634)
AXES = ("seq", "head")
GROUP = 4
ROWS = 8
VM = pl.BlockSpec(memory_space=pltpu.VMEM)
SM = pl.BlockSpec(memory_space=pltpu.SMEM)
ANY = pl.BlockSpec(memory_space=pl.ANY)
HBM = pl.BlockSpec(memory_space=pltpu.HBM)
ATTEND_VMEM = 24 * 2**20
OUT_VMEM = 12 * 2**20
CHUNKS = 2


def coords(i):
    s, h = divmod(i, 8)
    yl, r = divmod(s, 8)
    z, c = divmod(r, 2)
    x, yh = divmod(h, 2)
    return x, yh, yl, z, c


def index(x, yh, yl, z, c):
    return ((yl * 4 + z) * 2 + c) * 8 + x * 2 + yh


def move(array, dx=0, dyh=0, dyl=0, dz=0, dc=0):
    pairs = []
    for i in range(128):
        x, yh, yl, z, c = coords(i)
        pairs.append((i, index((x + dx) % 4, yh ^ dyh, yl ^ dyl, (z + dz) % 4, c ^ dc)))
    return lax.ppermute(array, AXES, pairs)


def normalize(h_ref, gain_ref):
    values = h_ref[...].astype(jnp.float32)
    spread = jnp.mean(values * values, axis=-1, keepdims=True)
    return (values * lax.rsqrt(spread + EPSILON) * gain_ref[...]).astype(jnp.bfloat16)


def keys_kernel(half_ref, h_ref, gain_ref, ko, vo, km, vm, kvo_ref, kvm_ref):
    normed = normalize(h_ref, gain_ref)
    for k_ref, v_ref, out_ref in ((ko, vo, kvo_ref), (km, vm, kvm_ref)):
        weight = jnp.concatenate([k_ref[0], v_ref[0]], axis=1)
        both = jnp.dot(normed, weight, preferred_element_type=jnp.float32)
        out_ref[...] = both.astype(jnp.bfloat16)


def queries_kernel(half_ref, h_ref, gain_ref, qm, qo, qm_ref, qo_ref):
    weight = jnp.concatenate([qm[0], qo[0]], axis=1)
    both = jnp.dot(normalize(h_ref, gain_ref), weight, preferred_element_type=jnp.float32)
    both = both.astype(jnp.bfloat16)
    qm_ref[...] = both[:, :HD]
    qo_ref[...] = both[:, HD:]


def project(kernel, operands, weight, half, parts, outs, vmem):
    rows, width = operands[0].shape
    block = 512

    def part(member, flip):
        return pl.BlockSpec((1, width, HD), lambda i, half: (member, 0, half[0] ^ flip))

    def rows_of(n):
        return pl.BlockSpec((block, n), lambda i, half: (i, 0))

    return pl.pallas_call(
        kernel,
        grid_spec=pltpu.PrefetchScalarGridSpec(
            num_scalar_prefetch=1,
            grid=(rows // block,),
            in_specs=[rows_of(width)]
            + [pl.BlockSpec((1, width), lambda i, half: (0, 0))] * (len(operands) - 1)
            + [part(*p) for p in parts],
            out_specs=[rows_of(n) for n in outs],
        ),
        out_shape=[jax.ShapeDtypeStruct((rows, n), jnp.bfloat16) for n in outs],
        compiler_params=pltpu.CompilerParams(vmem_limit_bytes=vmem),
        cost_estimate=pl.CostEstimate(flops=1024, bytes_accessed=1024, transcendentals=0),
        name="project",
    )(half, *operands, *[weight] * len(parts))


def gathered(kv_ref, list_ref, tile, group, half):
    parts = []
    for j in range(GROUP):
        row = pl.multiple_of(list_ref[tile, group * GROUP + j] * TILE, TILE)
        parts.append(kv_ref[pl.ds(row, TILE), half * HD : half * HD + HD])
    return jnp.concatenate(parts, axis=0)


def query_rows(tile):
    return pl.ds(pl.multiple_of(tile * TILE, TILE), TILE)


def score_tile(tile, groups, list_ref, count_ref, q_ref, kv_ref):
    q = q_ref[query_rows(tile), :]
    lane = lax.broadcasted_iota(jnp.int32, (TILE, GROUP * TILE), 1)
    out = []
    for g in range(groups):
        s = lax.dot_general(
            q, gathered(kv_ref, list_ref, tile, g, 0), (((1,), (1,)), ((), ())),
            preferred_element_type=jnp.float32,
        )
        out.append(jnp.where(lane < (count_ref[tile] - GROUP * g) * TILE, s, NEGATIVE))
    return out


def highest_of(scores):
    parts = [s[:, k : k + HD] for s in scores for k in range(0, GROUP * TILE, HD)]
    return jnp.max(functools.reduce(jnp.maximum, parts), axis=-1, keepdims=True)


def context_tile(tile, scores, highest, list_ref, kv_ref, o_ref):
    totals = summed = 0.0
    for g, s in enumerate(scores):
        weights = jnp.exp2((s - highest) * EXPONENT)
        for k in range(0, GROUP * TILE, HD):
            totals = totals + weights[:, k : k + HD]
        summed = summed + jnp.dot(
            weights.astype(jnp.bfloat16), gathered(kv_ref, list_ref, tile, g, 1),
            preferred_element_type=jnp.float32,
        )
    totals = jnp.sum(totals, axis=-1, keepdims=True)
    o_ref[query_rows(tile), :] = (summed / totals).astype(jnp.bfloat16)


def attend_kernel(list_ref, count_ref, order_ref, qm_ref, qp_ref, *rest):
    pieces, rest = rest[:16], rest[16:]
    outs, (kv_ref, q_ref, o_ref, sems) = rest[: 2 * CHUNKS], rest[2 * CHUNKS :]
    rows = pieces[0].shape[0]
    copies = [
        pltpu.make_async_copy(piece, kv_ref.at[pl.ds(k * rows, rows)], sems.at[k])
        for k, piece in enumerate(pieces)
    ]
    for copy in copies:
        copy.start()
    q_ref[:rows, :] = qm_ref[...]
    q_ref[rows:, :] = qp_ref[:rows, :]
    for copy in copies:
        copy.wait()
    tiles = q_ref.shape[0] // TILE

    @pl.loop(0, tiles // ROWS)
    def _(block):
        ids = [order_ref[block * ROWS + j] for j in range(ROWS)]
        longest = functools.reduce(jnp.maximum, [count_ref[t] for t in ids])
        needed = (longest + GROUP - 1) // GROUP
        for groups in range(1, SEL // GROUP + 1):

            @pl.when(needed == groups)
            def _():
                scores = [score_tile(t, groups, list_ref, count_ref, q_ref, kv_ref) for t in ids]
                tops = [highest_of(s) for s in scores]
                for t, s, top in zip(ids, scores, tops):
                    context_tile(t, s, top, list_ref, kv_ref, o_ref)


    part = outs[0].shape[0]
    for k, out in enumerate(outs):
        out[...] = o_ref[k * part : (k + 1) * part, :]


def attend(lists, counts, order, qm, qp, pieces):
    rows = qm.shape[0]
    part = jax.ShapeDtypeStruct((rows // CHUNKS, HD), jnp.bfloat16)
    return pl.pallas_call(
        attend_kernel,
        out_shape=[part] * (2 * CHUNKS),
        in_specs=[SM, SM, SM, VM, VM, HBM] + [ANY] * 15,
        out_specs=[VM] * (2 * CHUNKS),
        scratch_shapes=[
            pltpu.VMEM((16 * rows, 2 * HD), jnp.bfloat16),
            pltpu.VMEM((2 * rows, HD), jnp.bfloat16),
            pltpu.VMEM((2 * rows, HD), jnp.bfloat16),
            pltpu.SemaphoreType.DMA((16,)),
        ],
        compiler_params=pltpu.CompilerParams(vmem_limit_bytes=ATTEND_VMEM),
        cost_estimate=pl.CostEstimate(
            flops=4 * 2 * rows * SEL * TILE * HD, bytes_accessed=10 * 2**20,
            transcendentals=2 * rows * SEL * TILE,
        ),
        name="attend",
    )(lists, counts, order, qm, qp, *pieces)


def pack_weight(spot, weight, flip, held=None):
    rows = weight.shape[0]

    def kernel(spot_ref, weight_ref, *refs):
        out_ref = refs[-1]
        x, yh, yl = spot_ref[0], spot_ref[1], spot_ref[2]
        for i, d in enumerate((0, 1, 3, 2)):
            start = ((x + d) % 4 * 2 + (yh ^ flip)) * 256
            columns = pl.ds(pl.multiple_of(start, 256), 256)
            for r in range(rows // HD):
                taken = pl.ds(pl.multiple_of((r ^ yl) * HD, HD), HD)
                out_ref[r * HD : (r + 1) * HD, i * 256 : (i + 1) * 256] = weight_ref[taken, columns]
        if held is not None:
            out_ref[rows:, :] = refs[0][...]

    extra = [] if held is None else [held]
    return pl.pallas_call(
        kernel,
        in_specs=[SM] + [VM] * (1 + len(extra)),
        out_specs=VM,
        out_shape=jax.ShapeDtypeStruct((rows * (1 + len(extra)), 1024), weight.dtype),
        compiler_params=pltpu.CompilerParams(vmem_limit_bytes=OUT_VMEM),
        cost_estimate=pl.CostEstimate(flops=1024, bytes_accessed=1024, transcendentals=0),
        name="pack_weight",
    )(spot, weight, *extra)


def out_kernel(c0, c1, c2, c3, weight_ref, own_ref, plus_ref, minus_ref, up_ref, down_ref):
    context = jnp.concatenate([c0[...], c1[...], c2[...], c3[...]], axis=1)

    def product(k):
        part = weight_ref[:, 256 * k : 256 * (k + 1)]
        return jnp.dot(context, part, preferred_element_type=jnp.float32)

    far = product(3).astype(up_ref.dtype)
    half = up_ref.shape[0]
    up_ref[...] = far[:half]
    down_ref[...] = far[half:]
    for k, out in enumerate((own_ref, plus_ref, minus_ref)):
        out[...] = product(k)


def out_project(contexts, weight):
    rows = contexts[0].shape[0]
    return pl.pallas_call(
        out_kernel,
        in_specs=[VM] * 5,
        out_specs=[VM] * 5,
        out_shape=[jax.ShapeDtypeStruct((rows, 256), jnp.float32)] * 3
        + [jax.ShapeDtypeStruct((rows // 2, 256), jnp.bfloat16)] * 2,
        compiler_params=pltpu.CompilerParams(vmem_limit_bytes=OUT_VMEM),
        cost_estimate=pl.CostEstimate(
            flops=2 * rows * 512 * 1024, bytes_accessed=3 * 2**20, transcendentals=0
        ),
        name="out_project",
    )(*contexts, weight)


def sum_kernel(plus_ref, minus_ref, up_ref, down_ref, plus_out, minus_out):
    half = up_ref.shape[0]
    plus, minus = plus_ref[...], minus_ref[...]
    plus_out[:half, :] = (plus[:half] + up_ref[...].astype(jnp.float32)).astype(plus_out.dtype)
    plus_out[half:, :] = plus[half:].astype(plus_out.dtype)
    minus_out[:half, :] = minus[:half].astype(minus_out.dtype)
    lower = minus[half:] + down_ref[...].astype(jnp.float32)
    minus_out[half:, :] = lower.astype(minus_out.dtype)


def sum_blocks(plus, minus, up, down):
    return pl.pallas_call(
        sum_kernel,
        in_specs=[VM] * 4,
        out_specs=[VM] * 2,
        out_shape=[jax.ShapeDtypeStruct(plus.shape, jnp.bfloat16)] * 2,
        compiler_params=pltpu.CompilerParams(vmem_limit_bytes=OUT_VMEM),
        name="sum_blocks",
    )(plus, minus, up, down)


def finish_kernel(*refs):
    out_ref = refs[-1]
    rows = refs[0].shape[0]
    for k in range(2):
        own, *blocks = refs[3 * k : 3 * k + 3]
        total = own[...]
        for block in blocks:
            total = total + block[...].astype(jnp.float32)
        out_ref[k * rows : (k + 1) * rows, :] = total.astype(out_ref.dtype)


def finish(first, second):
    rows, columns = first[0].shape
    return pl.pallas_call(
        finish_kernel,
        in_specs=[VM] * 6,
        out_specs=VM,
        out_shape=jax.ShapeDtypeStruct((2 * rows, columns), jnp.bfloat16),
        compiler_params=pltpu.CompilerParams(vmem_limit_bytes=OUT_VMEM),
        name="finish",
    )(*first, *second)


def place_lists(tile, counts, yl, z, core):
    per_slab = tile.shape[0] // 2
    slab = tile // per_slab
    place = (((slab % 8 // 2 - z) % 4) * 2 + ((slab // 8) ^ yl)) * 2 + ((slab % 2) ^ core)
    lists = place * per_slab + tile % per_slab
    ids = jnp.arange(counts.shape[0], dtype=jnp.int32)
    before = (counts[None, :] > counts[:, None]) | (
        (counts[None, :] == counts[:, None]) & (ids[None, :] < ids[:, None])
    )
    rank = jnp.sum(before.astype(jnp.int32), axis=1)
    order = jnp.sum(jnp.where(rank[None, :] == ids[:, None], ids[None, :], 0), axis=1)
    return lists, counts, order


def per_device(hidden_states, norm_gain, qkv_weight, out_weight, selected_tiles, selected_count):
    rows_here = selected_tiles.shape[0]
    seq = lax.axis_index("seq")
    head = lax.axis_index("head")
    yl, z, core = seq // 8, (seq % 8) // 2, seq % 2
    yh = head % 2

    x = head // 2
    spot = jnp.stack([x, yh, yl]).astype(jnp.int32)
    sent_weight = pack_weight(spot, out_weight, 1)

    barrier = lax.optimization_barrier
    half = jnp.reshape(yl, (1,)).astype(jnp.int32)
    gain = norm_gain.reshape(1, -1)
    kvo, kvm = project(
        keys_kernel, (hidden_states, gain), qkv_weight, half,
        ((1, 1), (2, 1), (1, 0), (2, 0)), (2 * HD, 2 * HD), 60 * 2**20,
    )
    qm, qo = project(
        queries_kernel, (hidden_states, gain), qkv_weight, half,
        ((0, 0), (0, 1)), (HD, HD), 24 * 2**20,
    )

    kvp = move(kvo, dyl=1)
    first, kvo = barrier((selected_count, kvo))
    kvm, first = barrier((kvm, move(first, dc=1)))
    up_m, down_m, core_m = move(kvm, dz=1), move(kvm, dz=-1), move(kvm, dc=1)
    kvp, sent_weight, first = barrier((kvp, sent_weight, first))
    up_p, down_p = move(kvp, dz=1), move(kvp, dz=-1)
    other_weight = move(sent_weight, dyh=1)
    core_up_m, core_down_m = move(up_m, dc=1), move(down_m, dc=1)
    counts = jnp.maximum(selected_count, jnp.minimum(first, 1))
    packed = jnp.concatenate(
        [selected_tiles, counts[:, None], jnp.zeros((rows_here, 95), jnp.int32)], axis=1
    )
    sent_queries = jnp.concatenate([qo, packed.astype(jnp.bfloat16)], axis=0)
    up_m, down_m, up_p, down_p, sent_queries, core_m, core_up_m, core_down_m, other_weight = barrier(
        (up_m, down_m, up_p, down_p, sent_queries, core_m, core_up_m, core_down_m, other_weight)
    )
    far_m, far_p = move(up_m, dz=1), move(down_p, dz=-1)
    qp = move(sent_queries, dyl=1)
    qp, up_p, down_p, own_p = barrier((qp, up_p, down_p, kvp))
    packed_p = qp[qo.shape[0] :].astype(jnp.int32)
    core_p = move(own_p, dc=1)
    core_up_p, core_down_p = move(up_p, dc=1), move(down_p, dc=1)
    packed = jnp.concatenate([packed, packed_p], axis=0)
    lists, counts, order = place_lists(packed[:, :SEL], packed[:, SEL], yl, z, core)
    far_m, far_p, core_p, core_up_p, core_down_p, lists, counts, order = barrier(
        (far_m, far_p, core_p, core_up_p, core_down_p, lists, counts, order)
    )
    core_far_m, core_far_p = move(far_m, dc=1), move(far_p, dc=1)
    parts = attend(
        lists, counts, order, qm, qp,
        (kvm, core_m, kvp, core_p, down_m, core_down_m, down_p, core_down_p,
         far_m, core_far_m, far_p, core_far_p, up_m, core_up_m, up_p, core_up_p),
    )

    *parts, out_weight = barrier((*parts, out_weight))
    weight = pack_weight(spot, out_weight, 0, other_weight)
    contexts = [
        (mine, move(partner, dyl=1), move(mine, dyh=1), move(partner, dyl=1, dyh=1))
        for mine, partner in zip(parts[:CHUNKS], parts[CHUNKS:])
    ]
    done = []
    for held in contexts:
        own, plus, minus, up, down = out_project(held, weight)
        plus, minus = sum_blocks(plus, minus, move(up, dx=1), move(down, dx=-1))
        done.append((own, move(plus, dx=1), move(minus, dx=-1)))
    return finish(*done)


def solution(mesh):
    return jax.shard_map(
        per_device,
        mesh=mesh,
        in_specs=(
            P("seq", None),
            P(),
            P(None, None, "head"),
            P("head", None),
            P("seq", None),
            P("seq"),
        ),
        out_specs=P("seq", "head"),
        check_vma=False,
    )
```

```python
import functools

import jax
import jax.numpy as jnp
from jax import lax
from jax.experimental import pallas as pl
from jax.experimental.pallas import tpu as pltpu
from jax.sharding import PartitionSpec as P

D = 2048
HD = 128
TILE = 64
SEL = 32
EPSILON = 1e-06
NEGATIVE = -1e30
EXPONENT = float(HD**-0.5 * 1.4426950408889634)
AXES = ("seq", "head")
GROUP = 4
ROWS = 8
VM = pl.BlockSpec(memory_space=pltpu.VMEM)
SM = pl.BlockSpec(memory_space=pltpu.SMEM)
ANY = pl.BlockSpec(memory_space=pl.ANY)
HBM = pl.BlockSpec(memory_space=pltpu.HBM)
ATTEND_VMEM = 24 * 2**20
OUT_VMEM = 12 * 2**20
CHUNKS = 2


def coords(i):
    s, h = divmod(i, 8)
    yl, r = divmod(s, 8)
    z, c = divmod(r, 2)
    x, yh = divmod(h, 2)
    return x, yh, yl, z, c


def index(x, yh, yl, z, c):
    return ((yl * 4 + z) * 2 + c) * 8 + x * 2 + yh


def move(array, dx=0, dyh=0, dyl=0, dz=0, dc=0):
    pairs = []
    for i in range(128):
        x, yh, yl, z, c = coords(i)
        pairs.append((i, index((x + dx) % 4, yh ^ dyh, yl ^ dyl, (z + dz) % 4, c ^ dc)))
    return lax.ppermute(array, AXES, pairs)


def normalize(h_ref, gain_ref):
    values = h_ref[...].astype(jnp.float32)
    spread = jnp.mean(values * values, axis=-1, keepdims=True)
    return (values * lax.rsqrt(spread + EPSILON) * gain_ref[...]).astype(jnp.bfloat16)


def keys_kernel(half_ref, h_ref, gain_ref, ko, vo, km, vm, kvo_ref, kvm_ref):
    normed = normalize(h_ref, gain_ref)
    for k_ref, v_ref, out_ref in ((ko, vo, kvo_ref), (km, vm, kvm_ref)):
        weight = jnp.concatenate([k_ref[0], v_ref[0]], axis=1)
        both = jnp.dot(normed, weight, preferred_element_type=jnp.float32)
        out_ref[...] = both.astype(jnp.bfloat16)


def queries_kernel(half_ref, h_ref, gain_ref, qm, qo, qm_ref, qo_ref):
    weight = jnp.concatenate([qm[0], qo[0]], axis=1)
    both = jnp.dot(normalize(h_ref, gain_ref), weight, preferred_element_type=jnp.float32)
    both = both.astype(jnp.bfloat16)
    qm_ref[...] = both[:, :HD]
    qo_ref[...] = both[:, HD:]


def project(kernel, operands, weight, half, parts, outs, vmem):
    rows, width = operands[0].shape
    block = 512

    def part(member, flip):
        return pl.BlockSpec((1, width, HD), lambda i, half: (member, 0, half[0] ^ flip))

    def rows_of(n):
        return pl.BlockSpec((block, n), lambda i, half: (i, 0))

    return pl.pallas_call(
        kernel,
        grid_spec=pltpu.PrefetchScalarGridSpec(
            num_scalar_prefetch=1,
            grid=(rows // block,),
            in_specs=[rows_of(width)]
            + [pl.BlockSpec((1, width), lambda i, half: (0, 0))] * (len(operands) - 1)
            + [part(*p) for p in parts],
            out_specs=[rows_of(n) for n in outs],
        ),
        out_shape=[jax.ShapeDtypeStruct((rows, n), jnp.bfloat16) for n in outs],
        compiler_params=pltpu.CompilerParams(vmem_limit_bytes=vmem),
        cost_estimate=pl.CostEstimate(flops=1024, bytes_accessed=1024, transcendentals=0),
        name="project",
    )(half, *operands, *[weight] * len(parts))


def gathered(kv_ref, list_ref, tile, group, half):
    parts = []
    for j in range(GROUP):
        row = pl.multiple_of(list_ref[tile, group * GROUP + j] * TILE, TILE)
        parts.append(kv_ref[pl.ds(row, TILE), half * HD : half * HD + HD])
    return jnp.concatenate(parts, axis=0)


def query_rows(tile):
    return pl.ds(pl.multiple_of(tile * TILE, TILE), TILE)


def score_tile(tile, groups, list_ref, count_ref, q_ref, kv_ref):
    q = q_ref[query_rows(tile), :]
    lane = lax.broadcasted_iota(jnp.int32, (1, GROUP * TILE), 1)
    out = []
    for g in range(groups):
        s = lax.dot_general(
            q, gathered(kv_ref, list_ref, tile, g, 0), (((1,), (1,)), ((), ())),
            preferred_element_type=jnp.float32,
        )
        usable = lane < (count_ref[tile] - GROUP * g) * TILE
        out.append(jnp.minimum(s, jnp.where(usable, -NEGATIVE, NEGATIVE)))
    return out


def highest_of(scores):
    parts = [s[:, k : k + HD] for s in scores for k in range(0, GROUP * TILE, HD)]
    return jnp.max(functools.reduce(jnp.maximum, parts), axis=-1, keepdims=True)


def context_tile(tile, scores, highest, list_ref, kv_ref, o_ref):
    totals = summed = 0.0
    for g, s in enumerate(scores):
        weights = jnp.exp2((s - highest) * EXPONENT)
        for k in range(0, GROUP * TILE, HD):
            totals = totals + weights[:, k : k + HD]
        summed = summed + jnp.dot(
            weights.astype(jnp.bfloat16), gathered(kv_ref, list_ref, tile, g, 1),
            preferred_element_type=jnp.float32,
        )
    totals = jnp.sum(totals, axis=-1, keepdims=True)
    o_ref[query_rows(tile), :] = (summed / totals).astype(jnp.bfloat16)


def attend_kernel(list_ref, count_ref, order_ref, qm_ref, qp_ref, *rest):
    pieces, rest = rest[:16], rest[16:]
    outs, (kv_ref, q_ref, o_ref, sems) = rest[: 2 * CHUNKS], rest[2 * CHUNKS :]
    rows = pieces[0].shape[0]
    copies = [
        pltpu.make_async_copy(piece, kv_ref.at[pl.ds(k * rows, rows)], sems.at[k])
        for k, piece in enumerate(pieces)
    ]
    for copy in copies:
        copy.start()
    q_ref[:rows, :] = qm_ref[...]
    q_ref[rows:, :] = qp_ref[:rows, :]
    for copy in copies:
        copy.wait()
    tiles = q_ref.shape[0] // TILE

    @pl.loop(0, tiles // ROWS)
    def _(block):
        ids = [order_ref[block * ROWS + j] for j in range(ROWS)]
        longest = functools.reduce(jnp.maximum, [count_ref[t] for t in ids])
        needed = (longest + GROUP - 1) // GROUP
        for groups in range(1, SEL // GROUP + 1):

            @pl.when(needed == groups)
            def _():
                scores = [score_tile(t, groups, list_ref, count_ref, q_ref, kv_ref) for t in ids]
                tops = [highest_of(s) for s in scores]
                for t, s, top in zip(ids, scores, tops):
                    context_tile(t, s, top, list_ref, kv_ref, o_ref)


    part = outs[0].shape[0]
    for k, out in enumerate(outs):
        out[...] = o_ref[k * part : (k + 1) * part, :]


def attend(lists, counts, order, qm, qp, pieces):
    rows = qm.shape[0]
    part = jax.ShapeDtypeStruct((rows // CHUNKS, HD), jnp.bfloat16)
    return pl.pallas_call(
        attend_kernel,
        out_shape=[part] * (2 * CHUNKS),
        in_specs=[SM, SM, SM, VM, VM, HBM] + [ANY] * 15,
        out_specs=[VM] * (2 * CHUNKS),
        scratch_shapes=[
            pltpu.VMEM((16 * rows, 2 * HD), jnp.bfloat16),
            pltpu.VMEM((2 * rows, HD), jnp.bfloat16),
            pltpu.VMEM((2 * rows, HD), jnp.bfloat16),
            pltpu.SemaphoreType.DMA((16,)),
        ],
        compiler_params=pltpu.CompilerParams(vmem_limit_bytes=ATTEND_VMEM),
        cost_estimate=pl.CostEstimate(
            flops=4 * 2 * rows * SEL * TILE * HD, bytes_accessed=10 * 2**20,
            transcendentals=2 * rows * SEL * TILE,
        ),
        name="attend",
    )(lists, counts, order, qm, qp, *pieces)


def pack_weight(spot, weight, flip, held=None):
    rows = weight.shape[0]

    def kernel(spot_ref, weight_ref, *refs):
        out_ref = refs[-1]
        x, yh, yl = spot_ref[0], spot_ref[1], spot_ref[2]
        for i, d in enumerate((0, 1, 3, 2)):
            start = ((x + d) % 4 * 2 + (yh ^ flip)) * 256
            columns = pl.ds(pl.multiple_of(start, 256), 256)
            for r in range(rows // HD):
                taken = pl.ds(pl.multiple_of((r ^ yl) * HD, HD), HD)
                out_ref[r * HD : (r + 1) * HD, i * 256 : (i + 1) * 256] = weight_ref[taken, columns]
        if held is not None:
            out_ref[rows:, :] = refs[0][...]

    extra = [] if held is None else [held]
    return pl.pallas_call(
        kernel,
        in_specs=[SM] + [VM] * (1 + len(extra)),
        out_specs=VM,
        out_shape=jax.ShapeDtypeStruct((rows * (1 + len(extra)), 1024), weight.dtype),
        compiler_params=pltpu.CompilerParams(vmem_limit_bytes=OUT_VMEM),
        cost_estimate=pl.CostEstimate(flops=1024, bytes_accessed=1024, transcendentals=0),
        name="pack_weight",
    )(spot, weight, *extra)


def out_kernel(c0, c1, c2, c3, weight_ref, own_ref, plus_ref, minus_ref, up_ref, down_ref):
    context = jnp.concatenate([c0[...], c1[...], c2[...], c3[...]], axis=1)

    def product(k):
        part = weight_ref[:, 256 * k : 256 * (k + 1)]
        return jnp.dot(context, part, preferred_element_type=jnp.float32)

    far = product(3).astype(up_ref.dtype)
    half = up_ref.shape[0]
    up_ref[...] = far[:half]
    down_ref[...] = far[half:]
    for k, out in enumerate((own_ref, plus_ref, minus_ref)):
        out[...] = product(k)


def out_project(contexts, weight):
    rows = contexts[0].shape[0]
    return pl.pallas_call(
        out_kernel,
        in_specs=[VM] * 5,
        out_specs=[VM] * 5,
        out_shape=[jax.ShapeDtypeStruct((rows, 256), jnp.float32)] * 3
        + [jax.ShapeDtypeStruct((rows // 2, 256), jnp.bfloat16)] * 2,
        compiler_params=pltpu.CompilerParams(vmem_limit_bytes=OUT_VMEM),
        cost_estimate=pl.CostEstimate(
            flops=2 * rows * 512 * 1024, bytes_accessed=3 * 2**20, transcendentals=0
        ),
        name="out_project",
    )(*contexts, weight)


def sum_kernel(plus_ref, minus_ref, up_ref, down_ref, plus_out, minus_out):
    half = up_ref.shape[0]
    plus, minus = plus_ref[...], minus_ref[...]
    plus_out[:half, :] = (plus[:half] + up_ref[...].astype(jnp.float32)).astype(plus_out.dtype)
    plus_out[half:, :] = plus[half:].astype(plus_out.dtype)
    minus_out[:half, :] = minus[:half].astype(minus_out.dtype)
    lower = minus[half:] + down_ref[...].astype(jnp.float32)
    minus_out[half:, :] = lower.astype(minus_out.dtype)


def sum_blocks(plus, minus, up, down):
    return pl.pallas_call(
        sum_kernel,
        in_specs=[VM] * 4,
        out_specs=[VM] * 2,
        out_shape=[jax.ShapeDtypeStruct(plus.shape, jnp.bfloat16)] * 2,
        compiler_params=pltpu.CompilerParams(vmem_limit_bytes=OUT_VMEM),
        name="sum_blocks",
    )(plus, minus, up, down)


def finish_kernel(*refs):
    out_ref = refs[-1]
    rows = refs[0].shape[0]
    for k in range(2):
        own, *blocks = refs[3 * k : 3 * k + 3]
        total = own[...]
        for block in blocks:
            total = total + block[...].astype(jnp.float32)
        out_ref[k * rows : (k + 1) * rows, :] = total.astype(out_ref.dtype)


def finish(first, second):
    rows, columns = first[0].shape
    return pl.pallas_call(
        finish_kernel,
        in_specs=[VM] * 6,
        out_specs=VM,
        out_shape=jax.ShapeDtypeStruct((2 * rows, columns), jnp.bfloat16),
        compiler_params=pltpu.CompilerParams(vmem_limit_bytes=OUT_VMEM),
        name="finish",
    )(*first, *second)


def place_lists(tile, counts, yl, z, core):
    per_slab = tile.shape[0] // 2
    slab = tile // per_slab
    place = (((slab % 8 // 2 - z) % 4) * 2 + ((slab // 8) ^ yl)) * 2 + ((slab % 2) ^ core)
    lists = place * per_slab + tile % per_slab
    ids = jnp.arange(counts.shape[0], dtype=jnp.int32)
    before = (counts[None, :] > counts[:, None]) | (
        (counts[None, :] == counts[:, None]) & (ids[None, :] < ids[:, None])
    )
    rank = jnp.sum(before.astype(jnp.int32), axis=1)
    order = jnp.sum(jnp.where(rank[None, :] == ids[:, None], ids[None, :], 0), axis=1)
    return lists, counts, order


def per_device(hidden_states, norm_gain, qkv_weight, out_weight, selected_tiles, selected_count):
    rows_here = selected_tiles.shape[0]
    seq = lax.axis_index("seq")
    head = lax.axis_index("head")
    yl, z, core = seq // 8, (seq % 8) // 2, seq % 2
    yh = head % 2

    x = head // 2
    spot = jnp.stack([x, yh, yl]).astype(jnp.int32)
    sent_weight = pack_weight(spot, out_weight, 1)

    barrier = lax.optimization_barrier
    half = jnp.reshape(yl, (1,)).astype(jnp.int32)
    gain = norm_gain.reshape(1, -1)
    kvo, kvm = project(
        keys_kernel, (hidden_states, gain), qkv_weight, half,
        ((1, 1), (2, 1), (1, 0), (2, 0)), (2 * HD, 2 * HD), 60 * 2**20,
    )
    qm, qo = project(
        queries_kernel, (hidden_states, gain), qkv_weight, half,
        ((0, 0), (0, 1)), (HD, HD), 24 * 2**20,
    )

    kvp = move(kvo, dyl=1)
    first, kvo = barrier((selected_count, kvo))
    kvm, first = barrier((kvm, move(first, dc=1)))
    up_m, down_m, core_m = move(kvm, dz=1), move(kvm, dz=-1), move(kvm, dc=1)
    kvp, sent_weight, first = barrier((kvp, sent_weight, first))
    up_p, down_p = move(kvp, dz=1), move(kvp, dz=-1)
    other_weight = move(sent_weight, dyh=1)
    core_up_m, core_down_m = move(up_m, dc=1), move(down_m, dc=1)
    counts = jnp.maximum(selected_count, jnp.minimum(first, 1))
    packed = jnp.concatenate(
        [selected_tiles, counts[:, None], jnp.zeros((rows_here, 95), jnp.int32)], axis=1
    )
    sent_queries = jnp.concatenate([qo, packed.astype(jnp.bfloat16)], axis=0)
    up_m, down_m, up_p, down_p, sent_queries, core_m, core_up_m, core_down_m, other_weight = barrier(
        (up_m, down_m, up_p, down_p, sent_queries, core_m, core_up_m, core_down_m, other_weight)
    )
    far_m, far_p = move(up_m, dz=1), move(down_p, dz=-1)
    qp = move(sent_queries, dyl=1)
    qp, up_p, down_p, own_p = barrier((qp, up_p, down_p, kvp))
    packed_p = qp[qo.shape[0] :].astype(jnp.int32)
    core_p = move(own_p, dc=1)
    core_up_p, core_down_p = move(up_p, dc=1), move(down_p, dc=1)
    packed = jnp.concatenate([packed, packed_p], axis=0)
    lists, counts, order = place_lists(packed[:, :SEL], packed[:, SEL], yl, z, core)
    far_m, far_p, core_p, core_up_p, core_down_p, lists, counts, order = barrier(
        (far_m, far_p, core_p, core_up_p, core_down_p, lists, counts, order)
    )
    core_far_m, core_far_p = move(far_m, dc=1), move(far_p, dc=1)
    parts = attend(
        lists, counts, order, qm, qp,
        (kvm, core_m, kvp, core_p, down_m, core_down_m, down_p, core_down_p,
         far_m, core_far_m, far_p, core_far_p, up_m, core_up_m, up_p, core_up_p),
    )

    *parts, out_weight = barrier((*parts, out_weight))
    weight = pack_weight(spot, out_weight, 0, other_weight)
    contexts = [
        (mine, move(partner, dyl=1), move(mine, dyh=1), move(partner, dyl=1, dyh=1))
        for mine, partner in zip(parts[:CHUNKS], parts[CHUNKS:])
    ]
    done = []
    for held in contexts:
        own, plus, minus, up, down = out_project(held, weight)
        plus, minus = sum_blocks(plus, minus, move(up, dx=1), move(down, dx=-1))
        done.append((own, move(plus, dx=1), move(minus, dx=-1)))
    return finish(*done)


def solution(mesh):
    return jax.shard_map(
        per_device,
        mesh=mesh,
        in_specs=(
            P("seq", None),
            P(),
            P(None, None, "head"),
            P("head", None),
            P("seq", None),
            P("seq"),
        ),
        out_specs=P("seq", "head"),
        check_vma=False,
    )
```

```python
import functools

import jax
import jax.numpy as jnp
from jax import lax
from jax.experimental import pallas as pl
from jax.experimental.pallas import tpu as pltpu
from jax.sharding import PartitionSpec as P

D = 2048
HD = 128
TILE = 64
SEL = 32
EPSILON = 1e-06
NEGATIVE = -1e30
EXPONENT = float(HD**-0.5 * 1.4426950408889634)
AXES = ("seq", "head")
GROUP = 4
ROWS = 16
VM = pl.BlockSpec(memory_space=pltpu.VMEM)
SM = pl.BlockSpec(memory_space=pltpu.SMEM)
ANY = pl.BlockSpec(memory_space=pl.ANY)
HBM = pl.BlockSpec(memory_space=pltpu.HBM)
ATTEND_VMEM = 24 * 2**20
OUT_VMEM = 12 * 2**20
CHUNKS = 2


def coords(i):
    s, h = divmod(i, 8)
    yl, r = divmod(s, 8)
    z, c = divmod(r, 2)
    x, yh = divmod(h, 2)
    return x, yh, yl, z, c


def index(x, yh, yl, z, c):
    return ((yl * 4 + z) * 2 + c) * 8 + x * 2 + yh


def move(array, dx=0, dyh=0, dyl=0, dz=0, dc=0):
    pairs = []
    for i in range(128):
        x, yh, yl, z, c = coords(i)
        pairs.append((i, index((x + dx) % 4, yh ^ dyh, yl ^ dyl, (z + dz) % 4, c ^ dc)))
    return lax.ppermute(array, AXES, pairs)


def normalize(h_ref, gain_ref):
    values = h_ref[...].astype(jnp.float32)
    spread = jnp.mean(values * values, axis=-1, keepdims=True)
    return (values * lax.rsqrt(spread + EPSILON) * gain_ref[...]).astype(jnp.bfloat16)


def keys_kernel(half_ref, h_ref, gain_ref, ko, vo, km, vm, kvo_ref, kvm_ref):
    normed = normalize(h_ref, gain_ref)
    for k_ref, v_ref, out_ref in ((ko, vo, kvo_ref), (km, vm, kvm_ref)):
        weight = jnp.concatenate([k_ref[0], v_ref[0]], axis=1)
        both = jnp.dot(normed, weight, preferred_element_type=jnp.float32)
        out_ref[...] = both.astype(jnp.bfloat16)


def queries_kernel(half_ref, h_ref, gain_ref, qm, qo, qm_ref, qo_ref):
    weight = jnp.concatenate([qm[0], qo[0]], axis=1)
    both = jnp.dot(normalize(h_ref, gain_ref), weight, preferred_element_type=jnp.float32)
    both = both.astype(jnp.bfloat16)
    qm_ref[...] = both[:, :HD]
    qo_ref[...] = both[:, HD:]


def project(kernel, operands, weight, half, parts, outs, vmem):
    rows, width = operands[0].shape
    block = 512

    def part(member, flip):
        return pl.BlockSpec((1, width, HD), lambda i, half: (member, 0, half[0] ^ flip))

    def rows_of(n):
        return pl.BlockSpec((block, n), lambda i, half: (i, 0))

    return pl.pallas_call(
        kernel,
        grid_spec=pltpu.PrefetchScalarGridSpec(
            num_scalar_prefetch=1,
            grid=(rows // block,),
            in_specs=[rows_of(width)]
            + [pl.BlockSpec((1, width), lambda i, half: (0, 0))] * (len(operands) - 1)
            + [part(*p) for p in parts],
            out_specs=[rows_of(n) for n in outs],
        ),
        out_shape=[jax.ShapeDtypeStruct((rows, n), jnp.bfloat16) for n in outs],
        compiler_params=pltpu.CompilerParams(vmem_limit_bytes=vmem),
        cost_estimate=pl.CostEstimate(flops=1024, bytes_accessed=1024, transcendentals=0),
        name="project",
    )(half, *operands, *[weight] * len(parts))


def gathered(kv_ref, list_ref, tile, group, half):
    parts = []
    for j in range(GROUP):
        row = pl.multiple_of(list_ref[tile, group * GROUP + j] * TILE, TILE)
        parts.append(kv_ref[pl.ds(row, TILE), half * HD : half * HD + HD])
    return jnp.concatenate(parts, axis=0)


def query_rows(tile):
    return pl.ds(pl.multiple_of(tile * TILE, TILE), TILE)


def score_tile(tile, groups, list_ref, count_ref, q_ref, kv_ref):
    q = q_ref[query_rows(tile), :]
    lane = lax.broadcasted_iota(jnp.int32, (1, GROUP * TILE), 1)
    out = []
    for g in range(groups):
        s = lax.dot_general(
            q, gathered(kv_ref, list_ref, tile, g, 0), (((1,), (1,)), ((), ())),
            preferred_element_type=jnp.float32,
        )
        usable = lane < (count_ref[tile] - GROUP * g) * TILE
        out.append(jnp.minimum(s, jnp.where(usable, -NEGATIVE, NEGATIVE)))
    return out


def highest_of(scores):
    parts = [s[:, k : k + HD] for s in scores for k in range(0, GROUP * TILE, HD)]
    return jnp.max(functools.reduce(jnp.maximum, parts), axis=-1, keepdims=True)


def context_tile(tile, scores, highest, list_ref, kv_ref, o_ref):
    totals = summed = 0.0
    for g, s in enumerate(scores):
        weights = jnp.exp2((s - highest) * EXPONENT)
        for k in range(0, GROUP * TILE, HD):
            totals = totals + weights[:, k : k + HD]
        summed = summed + jnp.dot(
            weights.astype(jnp.bfloat16), gathered(kv_ref, list_ref, tile, g, 1),
            preferred_element_type=jnp.float32,
        )
    totals = jnp.sum(totals, axis=-1, keepdims=True)
    o_ref[query_rows(tile), :] = (summed * (1.0 / totals)).astype(jnp.bfloat16)


def attend_kernel(list_ref, count_ref, order_ref, qm_ref, qp_ref, *rest):
    pieces, rest = rest[:16], rest[16:]
    outs, (kv_ref, q_ref, o_ref, sems) = rest[: 2 * CHUNKS], rest[2 * CHUNKS :]
    rows = pieces[0].shape[0]
    copies = [
        pltpu.make_async_copy(piece, kv_ref.at[pl.ds(k * rows, rows)], sems.at[k])
        for k, piece in enumerate(pieces)
    ]
    for copy in copies:
        copy.start()
    q_ref[:rows, :] = qm_ref[...]
    q_ref[rows:, :] = qp_ref[:rows, :]
    for copy in copies:
        copy.wait()
    tiles = q_ref.shape[0] // TILE

    @pl.loop(0, tiles // ROWS)
    def _(block):
        ids = [order_ref[block * ROWS + j] for j in range(ROWS)]
        longest = functools.reduce(jnp.maximum, [count_ref[t] for t in ids])
        needed = (longest + GROUP - 1) // GROUP
        for groups in range(1, SEL // GROUP + 1):

            @pl.when(needed == groups)
            def _():
                scores = [score_tile(t, groups, list_ref, count_ref, q_ref, kv_ref) for t in ids]
                tops = [highest_of(s) for s in scores]
                for t, s, top in zip(ids, scores, tops):
                    context_tile(t, s, top, list_ref, kv_ref, o_ref)


    part = outs[0].shape[0]
    for k, out in enumerate(outs):
        out[...] = o_ref[k * part : (k + 1) * part, :]


def attend(lists, counts, order, qm, qp, pieces):
    rows = qm.shape[0]
    part = jax.ShapeDtypeStruct((rows // CHUNKS, HD), jnp.bfloat16)
    return pl.pallas_call(
        attend_kernel,
        out_shape=[part] * (2 * CHUNKS),
        in_specs=[SM, SM, SM, VM, VM, HBM] + [ANY] * 15,
        out_specs=[VM] * (2 * CHUNKS),
        scratch_shapes=[
            pltpu.VMEM((16 * rows, 2 * HD), jnp.bfloat16),
            pltpu.VMEM((2 * rows, HD), jnp.bfloat16),
            pltpu.VMEM((2 * rows, HD), jnp.bfloat16),
            pltpu.SemaphoreType.DMA((16,)),
        ],
        compiler_params=pltpu.CompilerParams(vmem_limit_bytes=ATTEND_VMEM),
        cost_estimate=pl.CostEstimate(
            flops=4 * 2 * rows * SEL * TILE * HD, bytes_accessed=10 * 2**20,
            transcendentals=2 * rows * SEL * TILE,
        ),
        name="attend",
    )(lists, counts, order, qm, qp, *pieces)


def pack_weight(spot, weight, flip, held=None):
    rows = weight.shape[0]

    def kernel(spot_ref, weight_ref, *refs):
        out_ref = refs[-1]
        x, yh, yl = spot_ref[0], spot_ref[1], spot_ref[2]
        for i, d in enumerate((0, 1, 3, 2)):
            start = ((x + d) % 4 * 2 + (yh ^ flip)) * 256
            columns = pl.ds(pl.multiple_of(start, 256), 256)
            for r in range(rows // HD):
                taken = pl.ds(pl.multiple_of((r ^ yl) * HD, HD), HD)
                out_ref[r * HD : (r + 1) * HD, i * 256 : (i + 1) * 256] = weight_ref[taken, columns]
        if held is not None:
            out_ref[rows:, :] = refs[0][...]

    extra = [] if held is None else [held]
    return pl.pallas_call(
        kernel,
        in_specs=[SM] + [VM] * (1 + len(extra)),
        out_specs=VM,
        out_shape=jax.ShapeDtypeStruct((rows * (1 + len(extra)), 1024), weight.dtype),
        compiler_params=pltpu.CompilerParams(vmem_limit_bytes=OUT_VMEM),
        cost_estimate=pl.CostEstimate(flops=1024, bytes_accessed=1024, transcendentals=0),
        name="pack_weight",
    )(spot, weight, *extra)


def out_kernel(c0, c1, c2, c3, weight_ref, own_ref, plus_ref, minus_ref, up_ref, down_ref):
    context = jnp.concatenate([c0[...], c1[...], c2[...], c3[...]], axis=1)

    def product(k):
        part = weight_ref[:, 256 * k : 256 * (k + 1)]
        return jnp.dot(context, part, preferred_element_type=jnp.float32)

    far = product(3).astype(up_ref.dtype)
    half = up_ref.shape[0]
    up_ref[...] = far[:half]
    down_ref[...] = far[half:]
    for k, out in enumerate((own_ref, plus_ref, minus_ref)):
        out[...] = product(k)


def out_project(contexts, weight):
    rows = contexts[0].shape[0]
    return pl.pallas_call(
        out_kernel,
        in_specs=[VM] * 5,
        out_specs=[VM] * 5,
        out_shape=[jax.ShapeDtypeStruct((rows, 256), jnp.float32)] * 3
        + [jax.ShapeDtypeStruct((rows // 2, 256), jnp.bfloat16)] * 2,
        compiler_params=pltpu.CompilerParams(vmem_limit_bytes=OUT_VMEM),
        cost_estimate=pl.CostEstimate(
            flops=2 * rows * 512 * 1024, bytes_accessed=3 * 2**20, transcendentals=0
        ),
        name="out_project",
    )(*contexts, weight)


def sum_kernel(plus_ref, minus_ref, up_ref, down_ref, plus_out, minus_out):
    half = up_ref.shape[0]
    plus, minus = plus_ref[...], minus_ref[...]
    plus_out[:half, :] = (plus[:half] + up_ref[...].astype(jnp.float32)).astype(plus_out.dtype)
    plus_out[half:, :] = plus[half:].astype(plus_out.dtype)
    minus_out[:half, :] = minus[:half].astype(minus_out.dtype)
    lower = minus[half:] + down_ref[...].astype(jnp.float32)
    minus_out[half:, :] = lower.astype(minus_out.dtype)


def sum_blocks(plus, minus, up, down):
    return pl.pallas_call(
        sum_kernel,
        in_specs=[VM] * 4,
        out_specs=[VM] * 2,
        out_shape=[jax.ShapeDtypeStruct(plus.shape, jnp.bfloat16)] * 2,
        compiler_params=pltpu.CompilerParams(vmem_limit_bytes=OUT_VMEM),
        name="sum_blocks",
    )(plus, minus, up, down)


def finish_kernel(*refs):
    out_ref = refs[-1]
    rows = refs[0].shape[0]
    for k in range(2):
        own, *blocks = refs[3 * k : 3 * k + 3]
        total = own[...]
        for block in blocks:
            total = total + block[...].astype(jnp.float32)
        out_ref[k * rows : (k + 1) * rows, :] = total.astype(out_ref.dtype)


def finish(first, second):
    rows, columns = first[0].shape
    return pl.pallas_call(
        finish_kernel,
        in_specs=[VM] * 6,
        out_specs=VM,
        out_shape=jax.ShapeDtypeStruct((2 * rows, columns), jnp.bfloat16),
        compiler_params=pltpu.CompilerParams(vmem_limit_bytes=OUT_VMEM),
        name="finish",
    )(*first, *second)


def place_lists(tile, counts, yl, z, core):
    per_slab = tile.shape[0] // 2
    slab = tile // per_slab
    place = (((slab % 8 // 2 - z) % 4) * 2 + ((slab // 8) ^ yl)) * 2 + ((slab % 2) ^ core)
    lists = place * per_slab + tile % per_slab
    ids = jnp.arange(counts.shape[0], dtype=jnp.int32)
    before = (counts[None, :] > counts[:, None]) | (
        (counts[None, :] == counts[:, None]) & (ids[None, :] < ids[:, None])
    )
    rank = jnp.sum(before.astype(jnp.int32), axis=1)
    order = jnp.sum(jnp.where(rank[None, :] == ids[:, None], ids[None, :], 0), axis=1)
    return lists, counts, order


def per_device(hidden_states, norm_gain, qkv_weight, out_weight, selected_tiles, selected_count):
    rows_here = selected_tiles.shape[0]
    seq = lax.axis_index("seq")
    head = lax.axis_index("head")
    yl, z, core = seq // 8, (seq % 8) // 2, seq % 2
    yh = head % 2

    x = head // 2
    spot = jnp.stack([x, yh, yl]).astype(jnp.int32)
    sent_weight = pack_weight(spot, out_weight, 1)

    barrier = lax.optimization_barrier
    half = jnp.reshape(yl, (1,)).astype(jnp.int32)
    gain = norm_gain.reshape(1, -1)
    kvo, kvm = project(
        keys_kernel, (hidden_states, gain), qkv_weight, half,
        ((1, 1), (2, 1), (1, 0), (2, 0)), (2 * HD, 2 * HD), 60 * 2**20,
    )
    qm, qo = project(
        queries_kernel, (hidden_states, gain), qkv_weight, half,
        ((0, 0), (0, 1)), (HD, HD), 24 * 2**20,
    )

    kvp = move(kvo, dyl=1)
    first, kvo = barrier((selected_count, kvo))
    kvm, first = barrier((kvm, move(first, dc=1)))
    up_m, down_m, core_m = move(kvm, dz=1), move(kvm, dz=-1), move(kvm, dc=1)
    kvp, sent_weight, first = barrier((kvp, sent_weight, first))
    up_p, down_p = move(kvp, dz=1), move(kvp, dz=-1)
    other_weight = move(sent_weight, dyh=1)
    core_up_m, core_down_m = move(up_m, dc=1), move(down_m, dc=1)
    counts = jnp.maximum(selected_count, jnp.minimum(first, 1))
    packed = jnp.concatenate(
        [selected_tiles, counts[:, None], jnp.zeros((rows_here, 95), jnp.int32)], axis=1
    )
    sent_queries = jnp.concatenate([qo, packed.astype(jnp.bfloat16)], axis=0)
    up_m, down_m, up_p, down_p, sent_queries, core_m, core_up_m, core_down_m, other_weight = barrier(
        (up_m, down_m, up_p, down_p, sent_queries, core_m, core_up_m, core_down_m, other_weight)
    )
    far_m, far_p = move(up_m, dz=1), move(down_p, dz=-1)
    qp = move(sent_queries, dyl=1)
    qp, up_p, down_p, own_p = barrier((qp, up_p, down_p, kvp))
    packed_p = qp[qo.shape[0] :].astype(jnp.int32)
    core_p = move(own_p, dc=1)
    core_up_p, core_down_p = move(up_p, dc=1), move(down_p, dc=1)
    packed = jnp.concatenate([packed, packed_p], axis=0)
    lists, counts, order = place_lists(packed[:, :SEL], packed[:, SEL], yl, z, core)
    far_m, far_p, core_p, core_up_p, core_down_p, lists, counts, order = barrier(
        (far_m, far_p, core_p, core_up_p, core_down_p, lists, counts, order)
    )
    core_far_m, core_far_p = move(far_m, dc=1), move(far_p, dc=1)
    parts = attend(
        lists, counts, order, qm, qp,
        (kvm, core_m, kvp, core_p, down_m, core_down_m, down_p, core_down_p,
         far_m, core_far_m, far_p, core_far_p, up_m, core_up_m, up_p, core_up_p),
    )

    *parts, out_weight = barrier((*parts, out_weight))
    weight = pack_weight(spot, out_weight, 0, other_weight)
    contexts = [
        (mine, move(partner, dyl=1), move(mine, dyh=1), move(partner, dyl=1, dyh=1))
        for mine, partner in zip(parts[:CHUNKS], parts[CHUNKS:])
    ]
    done = []
    for held in contexts:
        own, plus, minus, up, down = out_project(held, weight)
        plus, minus = sum_blocks(plus, minus, move(up, dx=1), move(down, dx=-1))
        done.append((own, move(plus, dx=1), move(minus, dx=-1)))
    return finish(*done)


def solution(mesh):
    return jax.shard_map(
        per_device,
        mesh=mesh,
        in_specs=(
            P("seq", None),
            P(),
            P(None, None, "head"),
            P("head", None),
            P("seq", None),
            P("seq"),
        ),
        out_specs=P("seq", "head"),
        check_vma=False,
    )
```
